256 devices in a mesh: section: 4 (over x_hi, core), expert: 64 (over x_lo, y, z).
Axes of the slice: x: 4 (x_hi: 2, x_lo: 2; x = x_hi * 2 + x_lo), y: 4, z: 8, core: 2. Of those that a mesh axis runs over, the one named last changes fastest.
Arguments:
- layer_input: bfloat16 [2, 4, 8192, 2048], P(None, 'section', 'expert'), may hold values from -48 to 48
- entering: bfloat16 [4, 8192, 2048], P('section', 'expert'), may hold values from -6 to 6
- fresh: bfloat16 [1, 8192, 2048], P(None, 'expert'), may hold values from -6 to 6
- routes: int32 [2, 4, 8192, 2], P(None, 'section', 'expert'), may hold values from 0 to 63, all different within a row; in each aligned block of 128 rows (0 to 127, 128 to 255, ..., all dimensions but the last counted through in order) at most 6 rows name the same one
- gate_weights: bfloat16 [2, 4, 8192, 2], P(None, 'section', 'expert'), may hold values from 0.019897461 to 0.5
- norm_gain: float32 [4, 2048], P('section'), may hold values from 0.3 to 3
- w_gate: bfloat16 [4, 64, 2048, 768], P('section', 'expert'), may hold values from -0.125 to 0.125
- w_up: bfloat16 [4, 64, 2048, 768], P('section', 'expert'), may hold values from -0.125 to 0.125
- w_down: bfloat16 [4, 64, 768, 2048], P('section', 'expert'), may hold values from -0.21875 to 0.21875
Outputs:
- produced: bfloat16 [2, 4, 8192, 2048], P(None, 'section', 'expert')
The draws below stay inside these ranges and needn't reach their ends.
Inputs may be any that keep to these rules, and one draw needn't show every extreme that they name: `routes`: each row names 2 different experts; in each aligned block of 128 rows no expert is named more than 6 times, a bound that some block reaches.
All inputs are finite; a program needn't handle non-finite values.
Results may differ from the reference program's by a relative error of at most 0.0052.
Values may be sent and summed in bfloat16 or wider, within the bound.
A program may use at most 128 MiB of HBM per device.

```python
import math
import jax
import jax.numpy as jnp
import numpy as np
from jax import lax

D = 2048
FFE = 768
TOPK = 2
TICKS = 2
TOK_DEV = 128
SECTIONS = 4
EXPERTS = 64
TOKENS = 8192
SLOTS = 6
N_EXPERT = 64


def draw_layer_input(key, part):
    base_key, row_key, column_key = jax.random.split(key, 3)
    shape_all = (TICKS, SECTIONS, TOKENS, D)
    base_values = jnp.clip(jax.random.normal(base_key, shape_all, jnp.float32), -4.0, 4.0)
    row_scale = jnp.exp(jax.random.uniform(row_key, (TICKS, SECTIONS, TOKENS, 1), jnp.float32, math.log(0.3), math.log(3.0)))
    column_scale = jnp.exp(jax.random.uniform(column_key, (1, 1, 1, D), jnp.float32, math.log(0.4), math.log(4.0)))
    return (base_values * row_scale * column_scale).astype(jnp.bfloat16)


def level_of(key, dims, cuts, least, high):
    def one(axis_at, blocks):
        draws = jax.random.uniform(jax.random.fold_in(jax.random.fold_in(key, 6), axis_at), (blocks,), jnp.float32, least / len(cuts), high / len(cuts))
        return jnp.repeat(jnp.exp(draws), dims[axis_at] // blocks).reshape((-1,) + (1,) * (len(dims) - axis_at - 1))

    loudness = one(*cuts[0])
    for cut in cuts[1:]:
        loudness = loudness * one(*cut)
    return loudness


def routed_block(key, own, number, rows, number_of, top, reach, skew):
    ranking = jax.random.permutation(key, number_of)
    heavy_load, common = load_shares(number_of, rows * top, reach, skew, True), load_shares(number_of, rows * top, reach, skew, False)
    places = jnp.arange(number_of)

    def named(tallies, offset_by):
        used = int((tallies > 0).sum())
        fixed = max(1, used // 4)
        moved = fixed + (places - fixed + offset_by * (used - fixed)) % max(1, number_of - fixed)
        return jnp.zeros((number_of,), jnp.int32).at[ranking[jnp.where(places < fixed, places, moved)]].set(jnp.asarray(tallies, jnp.int32))

    tallies = jnp.where(number % 4 == 0, named(heavy_load, number // 4), named(common, number - number // 4 - 1))
    mixed = jax.random.permutation(jax.random.fold_in(own, 3), number_of)
    donor, receiver = mixed[0:number_of // 2 * 2:2], mixed[1:number_of // 2 * 2:2]
    margin = jnp.minimum(tallies[donor] - 1, reach - tallies[receiver]) // 2
    margin = jnp.where((donor == ranking[0]) | (receiver == ranking[0]) | (tallies[receiver] == 0), 0, jnp.maximum(margin, 0))
    moved = jax.random.randint(jax.random.fold_in(own, 4), (number_of // 2,), 0, 1 << 20) % (margin + 1)
    tallies = tallies.at[donor].add(-moved).at[receiver].add(moved)
    items = jnp.searchsorted(jnp.cumsum(tallies), jnp.arange(rows * top), side="right").astype(jnp.int32)
    grid = items.reshape(top, rows).T
    grid = grid[jax.random.permutation(jax.random.fold_in(own, 1), rows)]
    offset_by = jax.random.randint(jax.random.fold_in(own, 2), (rows, 1), 0, top)
    return jnp.take_along_axis(grid, (jnp.arange(top)[None, :] + offset_by) % top, axis=1)


def load_shares(number_of, total, reach, lean, full):
    portions = [(1 << 20) // math.isqrt(grade ** lean) + 1 for grade in range(1, number_of + 1)]
    largest = reach if full else min(reach, max(-(-total // number_of), total * portions[0] // sum(portions)))
    least = 1 if total - largest >= number_of - 1 else 0
    holding, spare = [largest] + [least] * (number_of - 1), total - largest - least * (number_of - 1)
    while spare > 0:
        movable = [i for i in range(1, number_of) if holding[i] < largest] or [i for i in range(1, number_of) if holding[i] < reach]
        mass, budget = sum([portions[i] for i in movable]), spare
        for i in movable:
            more = min(reach - holding[i], max(1, budget * portions[i] // mass), spare)
            holding[i] = holding[i] + more
            spare = spare - more
    return np.array(holding)


def noise(own_key, extent, spread, reach, cuts=(), held_as=jnp.bfloat16):
    values = jax.random.normal(own_key, extent, jnp.float32) * spread
    if len(cuts) > 0:
        values = level_of(own_key, extent, cuts, -0.22, 0.18) * values
    return jnp.clip(values, min=-reach, max=reach).astype(held_as)


def setup_inputs(seed: int = 0) -> dict:
    keys = jax.random.split(jax.random.key(seed), 10)
    layer_input = draw_layer_input(jax.random.fold_in(keys[9], 71), 0)
    entering = noise(keys[1], (SECTIONS, TOKENS, D), 1.0, 6.0, ((0, 4), (1, 64)))
    fresh = noise(keys[2], (TICKS - 1, TOKENS, D), 1.0, 6.0, ((1, 64),))
    routes_keys = jax.random.split(jax.random.fold_in(keys[3], 1), TICKS * SECTIONS * TOKENS // TOK_DEV)
    routes_turns = jax.random.permutation(jax.random.fold_in(keys[3], 3), TICKS * SECTIONS * TOKENS // TOK_DEV)
    routes = jax.vmap(lambda own, number: routed_block(jax.random.fold_in(keys[3], 2), own, number, TOK_DEV, EXPERTS, TOPK, SLOTS, 2))(routes_keys, routes_turns).reshape((TICKS, SECTIONS, TOKENS, TOPK))
    gate_weights = jnp.clip(jnp.exp(math.log(0.5) - 3.224016 * jax.random.uniform(keys[4], (TICKS, SECTIONS, TOKENS, TOPK), jnp.float32) ** level_of(keys[4], (TICKS, SECTIONS, TOKENS, TOPK), ((1, 4), (2, 64)), -0.2, 0.2)), 0.019897461, 0.5).astype(jnp.bfloat16)
    norm_gain = jnp.clip(jnp.exp(math.log(3.0) - 2.3025851 * jax.random.uniform(keys[5], (SECTIONS, D), jnp.float32) ** level_of(keys[5], (SECTIONS, D), ((0, 4),), -0.2, 0.2)), 0.3, 3.0)
    w_gate = noise(keys[6], (SECTIONS, EXPERTS, D, FFE), D ** -0.5, 0.125, ((0, 4), (1, 64)))
    w_up = noise(keys[7], (SECTIONS, EXPERTS, D, FFE), D ** -0.5, 0.125, ((0, 4), (1, 64)))
    w_down = noise(keys[8], (SECTIONS, EXPERTS, FFE, D), FFE ** -0.5, 0.21875, ((0, 4), (1, 64)))
    return {"layer_input": layer_input, "entering": entering, "fresh": fresh, "routes": routes, "gate_weights": gate_weights, "norm_gain": norm_gain, "w_gate": w_gate, "w_up": w_up, "w_down": w_down}


def contract_last(left, right):
    return lax.dot_general(left, right, (((1,), (1,)), ((), ())), preferred_element_type=jnp.float32)

def expert_backward(normed_rows, scaled_rows, gate_matrix, up_matrix, down_matrix):
    pre_gate = jnp.dot(normed_rows, gate_matrix, preferred_element_type=jnp.float32)
    pre_up = jnp.dot(normed_rows, up_matrix, preferred_element_type=jnp.float32)
    hidden_grad = contract_last(scaled_rows, down_matrix)
    sigmoid = jax.nn.sigmoid(pre_gate)
    gate_grad = (hidden_grad * pre_up * sigmoid * (1.0 + pre_gate * (1.0 - sigmoid))).astype(jnp.bfloat16)
    up_grad = (hidden_grad * pre_gate * sigmoid).astype(jnp.bfloat16)
    summed = contract_last(gate_grad, gate_matrix) + contract_last(up_grad, up_matrix)
    return summed.astype(jnp.bfloat16)

def layer_backward(layer_rows, incoming, route_rows, gate_rows, gain_row, gate_stack, up_stack, down_stack):
    xfloat = layer_rows.astype(jnp.float32)
    inverse = lax.rsqrt(lax.optimization_barrier(jnp.mean(xfloat * xfloat, axis=1, keepdims=True)) + 1e-05)
    normed = (xfloat * inverse * gain_row).astype(jnp.bfloat16)
    scaled = (gate_rows.astype(jnp.float32)[:, :, None] * incoming.astype(jnp.float32)[:, None, :]).astype(jnp.bfloat16)
    scaled = scaled.reshape(-1, D)
    flat_routes = route_rows.reshape(-1).astype(jnp.int32)
    assignments = flat_routes.shape[0]
    limit_rows = N_EXPERT * SLOTS

    def one_expert(collected, expert):
        picked = jnp.nonzero(flat_routes == expert, size=limit_rows, fill_value=assignments)[0].astype(jnp.int32)
        safe_index = jnp.minimum(picked, assignments - 1).astype(jnp.int32)
        result = expert_backward(normed[safe_index // TOPK], scaled[safe_index], gate_stack[expert], up_stack[expert], down_stack[expert])
        return (collected.at[picked].set(result, mode='drop'), None)
    collected, unused = lax.scan(one_expert, jnp.zeros((assignments, D), jnp.bfloat16), jnp.arange(EXPERTS, dtype=jnp.int32))
    normed_grad = lax.optimization_barrier(jnp.sum(collected.reshape(-1, TOPK, D).astype(jnp.float32), axis=1))
    weighted = gain_row * normed_grad
    project = lax.optimization_barrier(jnp.mean(xfloat * weighted, axis=1, keepdims=True))
    result = incoming.astype(jnp.float32) + inverse * weighted - xfloat * inverse ** 3 * project
    return result.astype(jnp.bfloat16)

def reference(layer_input, entering, fresh, routes, gate_weights, norm_gain, w_gate, w_up, w_down):
    produced = []
    for tick_index in range(TICKS):
        current = []
        for section_index in range(SECTIONS):
            if tick_index == 0:
                incoming = entering[section_index]
            elif section_index == SECTIONS - 1:
                incoming = fresh[tick_index - 1]
            else:
                incoming = produced[tick_index - 1][section_index + 1]
            current.append(layer_backward(layer_input[tick_index, section_index], incoming, routes[tick_index, section_index], gate_weights[tick_index, section_index], norm_gain[section_index], w_gate[section_index], w_up[section_index], w_down[section_index]))
        produced.append(current)
    return jnp.stack([jnp.stack(row_list, axis=0) for row_list in produced], axis=0)
```

```python
import functools

import jax
import jax.numpy as jnp
from jax import lax
from jax.experimental import pallas as pl
from jax.experimental.pallas import tpu as pltpu
from jax.sharding import PartitionSpec as P

D = 2048
FFE = 768
TICKS = 2
TOK = 128
PEERS = 64
SLOTS = 6
ROWS = PEERS * SLOTS
GROUPS = 8
IN_GROUP = PEERS // GROUPS
GROUP_ROWS = IN_GROUP * SLOTS
LANES = 128
TILES = D // LANES
RELAY = 4
RELAY_ROWS = TOK // RELAY
MESH = pl.DeviceIdType.MESH


def peer(me, i, sign):
    dx, dy, dz = i // 32, (i // 8) % 4, i % 8
    x, y, z = me // 32, (me // 8) % 4, me % 8
    return ((x + dx) % 2) * 32 + ((y + sign * dy + 4) % 4) * 8 + (z + sign * dz + 8) % 8


def lanes(c):
    return slice(c * LANES, (c + 1) * LANES)


def contract_last(left, right):
    return lax.dot_general(
        left, right, (((1,), (1,)), ((), ())), preferred_element_type=jnp.float32
    )


def kernel(
    tok_ref, gate_ref, slot_ref, x_ref, entering_ref, fresh_ref, gain_ref, wg_hbm, wu_hbm, wd_hbm,
    out_ref,
    wg, wu, wd, send_a, send_b, send_c, recv_a, recv_b, recv_c,
    by_token, by_slot, rows_a, rows_b, inverse_ref, current, arrived,
    w_sem, send_sem, recv_a_sem, recv_b_sem, recv_c_sem, relay_send_sem, relay_recv_sem,
):
    me = lax.axis_index("expert")
    section = lax.axis_index("section")
    last = lax.axis_size("section") - 1

    barrier = pltpu.get_barrier_semaphore()

    def greet(i, carry):
        pl.semaphore_signal(
            barrier, inc=1, device_id=(section, peer(me, i, 1)), device_id_type=MESH
        )
        return carry

    lax.fori_loop(1, PEERS, greet, 0)

    @pl.when(section < last)
    def _():
        pl.semaphore_signal(barrier, inc=1, device_id=(section + 1, me), device_id_type=MESH)

    weight_copies = [
        pltpu.make_async_copy(src, dst, w_sem.at[n])
        for n, (src, dst) in enumerate(((wg_hbm, wg), (wu_hbm, wu), (wd_hbm, wd)))
    ]
    for copy in weight_copies:
        copy.start()

    token_tiles = by_token.reshape(TOK + 1, TILES, LANES)
    by_token[pl.ds(TOK * TILES, TILES), :] = jnp.zeros((TILES, LANES), jnp.float32)

    def load_normed(tick):
        total = jnp.zeros((TOK, LANES), jnp.float32)
        for c in range(TILES):
            x = x_ref[tick, :, lanes(c)].astype(jnp.float32)
            total = total + x * x
        inverse = lax.rsqrt(jnp.sum(total, axis=1, keepdims=True) / D + 1e-05)
        inverse_ref[tick] = jnp.broadcast_to(inverse, (TOK, LANES))
        for c in range(TILES):
            x = x_ref[tick, :, lanes(c)].astype(jnp.float32)
            by_token[pl.ds(c, TOK, stride=TILES), :] = x * inverse * gain_ref[:, lanes(c)]

    def load_current():
        for c in range(TILES):
            by_token[pl.ds(c, TOK, stride=TILES), :] = current[:, lanes(c)].astype(jnp.float32)

    def ship(src, dst, s_sem, r_sem, i, sign):
        @pl.when(i == 0)
        def _():
            pltpu.make_async_copy(src.at[pl.ds(0, SLOTS)], dst.at[pl.ds(0, SLOTS)], r_sem).start()

        @pl.when(i > 0)
        def _():
            pltpu.make_async_remote_copy(
                src_ref=src.at[pl.ds(i * SLOTS, SLOTS)],
                dst_ref=dst.at[pl.ds(i * SLOTS, SLOTS)],
                send_sem=s_sem,
                recv_sem=r_sem,
                device_id=(section, peer(me, i, sign)),
                device_id_type=MESH,
            ).start()

    def pack_normed(tick):
        def body(i, carry):
            for r in range(SLOTS):
                s = i * SLOTS + r
                send_a[tick, s] = token_tiles[tok_ref[tick, s]].astype(jnp.bfloat16)
            return carry

        lax.fori_loop(0, PEERS, body, 0)

    def ship_normed(tick):
        def body(i, carry):
            ship(send_a.at[tick], recv_a.at[tick], send_sem.at[0, tick], recv_a_sem.at[tick, i // IN_GROUP], i, 1)
            return carry

        lax.fori_loop(0, PEERS, body, 0)

    def pack_and_ship_scaled(tick):
        def body(i, carry):
            for r in range(SLOTS):
                s = i * SLOTS + r
                send_b[tick, s] = (token_tiles[tok_ref[tick, s]] * gate_ref[tick, s]).astype(jnp.bfloat16)
            ship(send_b.at[tick], recv_b.at[tick], send_sem.at[1, tick], recv_b_sem.at[tick, i // IN_GROUP], i, 1)
            return carry

        lax.fori_loop(0, PEERS, body, 0)

    def wait_bytes(ref, sem):
        pltpu.make_async_copy(ref, ref, sem).wait()

    def to_rows(tiles, rows):
        by_slot[...] = tiles.astype(jnp.float32).reshape(GROUP_ROWS * TILES, LANES)
        for c in range(TILES):
            rows[:, lanes(c)] = by_slot[pl.ds(c, GROUP_ROWS, stride=TILES), :].astype(jnp.bfloat16)

    def experts(tick):
        def body(g, carry):
            part = pl.ds(g * GROUP_ROWS, GROUP_ROWS)
            wait_bytes(recv_a.at[tick, part], recv_a_sem.at[tick, g])
            wait_bytes(recv_b.at[tick, part], recv_b_sem.at[tick, g])
            to_rows(recv_a[tick, part], rows_a)
            to_rows(recv_b[tick, part], rows_b)
            normed = rows_a[...]
            pre_gate = jnp.dot(normed, wg[...], preferred_element_type=jnp.float32)
            pre_up = jnp.dot(normed, wu[...], preferred_element_type=jnp.float32)
            hidden_grad = contract_last(rows_b[...], wd[...])
            sigmoid = jax.nn.sigmoid(pre_gate)
            gate_grad = (
                hidden_grad * pre_up * sigmoid * (1.0 + pre_gate * (1.0 - sigmoid))
            ).astype(jnp.bfloat16)
            up_grad = (hidden_grad * pre_gate * sigmoid).astype(jnp.bfloat16)
            summed = contract_last(gate_grad, wg[...]) + contract_last(up_grad, wu[...])
            for c in range(TILES):
                by_slot[pl.ds(c, GROUP_ROWS, stride=TILES), :] = summed[:, lanes(c)]
            send_c[tick, part] = by_slot[...].reshape(GROUP_ROWS, TILES, LANES).astype(jnp.bfloat16)

            def give_back(j, inner):
                ship(send_c.at[tick], recv_c.at[tick], send_sem.at[2, tick], recv_c_sem.at[tick], g * IN_GROUP + j, -1)
                return inner

            lax.fori_loop(0, IN_GROUP, give_back, 0)
            return carry

        lax.fori_loop(0, GROUPS, body, 0)

    def combine(tick):
        wait_bytes(recv_c.at[tick], recv_c_sem.at[tick])

        def add(t, carry):
            by_token[pl.ds(pl.multiple_of(t * TILES, TILES), TILES), :] = recv_c[
                tick, slot_ref[tick, 0, t]
            ].astype(jnp.float32) + recv_c[tick, slot_ref[tick, 1, t]].astype(jnp.float32)
            return carry

        lax.fori_loop(0, TOK, add, 0)
        for part in range(RELAY):
            first = part * RELAY_ROWS
            rows = slice(first, first + RELAY_ROWS)
            total = jnp.zeros((RELAY_ROWS, LANES), jnp.float32)
            for c in range(TILES):
                weighted = gain_ref[:, lanes(c)] * by_token[pl.ds(first * TILES + c, RELAY_ROWS, stride=TILES), :]
                total = total + x_ref[tick, rows, lanes(c)].astype(jnp.float32) * weighted
            project = jnp.sum(total, axis=1, keepdims=True) / D
            inverse = inverse_ref[tick, rows]
            cubed = inverse * inverse * inverse * project
            for c in range(TILES):
                weighted = gain_ref[:, lanes(c)] * by_token[pl.ds(first * TILES + c, RELAY_ROWS, stride=TILES), :]
                out_ref[tick, rows, lanes(c)] = (
                    current[rows, lanes(c)].astype(jnp.float32)
                    + inverse * weighted
                    - x_ref[tick, rows, lanes(c)].astype(jnp.float32) * cubed
                ).astype(jnp.bfloat16)
            if tick == 0:

                @pl.when(section > 0)
                def _():
                    relay(part).start()

    def relay(part):
        rows = pl.ds(part * RELAY_ROWS, RELAY_ROWS)
        return pltpu.make_async_remote_copy(
            src_ref=out_ref.at[0, rows],
            dst_ref=arrived.at[rows],
            send_sem=relay_send_sem.at[part],
            recv_sem=relay_recv_sem.at[part],
            device_id=(section - 1, me),
            device_id_type=MESH,
        )

    load_normed(0)
    pack_normed(0)
    current[...] = entering_ref[...]
    load_current()

    @pl.when(section == 0)
    def _():
        pl.semaphore_wait(barrier, PEERS - 1)

    @pl.when(section > 0)
    def _():
        pl.semaphore_wait(barrier, PEERS)

    ship_normed(0)
    pack_and_ship_scaled(0)
    load_normed(1)
    pack_normed(1)
    for copy in weight_copies:
        copy.wait()
    experts(0)
    ship_normed(1)
    combine(0)

    @pl.when(section < last)
    def _():
        for part in range(RELAY):
            rows = pl.ds(part * RELAY_ROWS, RELAY_ROWS)
            pltpu.make_async_copy(arrived.at[rows], arrived.at[rows], relay_recv_sem.at[part]).wait()
        current[...] = arrived[...]

    @pl.when(section == last)
    def _():
        current[...] = fresh_ref[...]

    load_current()
    pack_and_ship_scaled(1)
    experts(1)
    combine(1)

    @pl.when(section > 0)
    def _():
        for part in range(RELAY):
            relay(part).wait_send()

    far = pl.ds(SLOTS, ROWS - SLOTS)
    for n, sent in enumerate((send_a, send_b, send_c)):
        for tick in range(TICKS):
            wait_bytes(sent.at[tick, far], send_sem.at[n, tick])


def local(layer_input, entering, fresh, routes, gate_weights, norm_gain, w_gate, w_up, w_down):
    me = lax.axis_index("expert")
    chosen = routes[:, 0].reshape(TICKS, -1)
    order = jnp.arange(2 * TOK, dtype=jnp.int32)
    same = (chosen[:, :, None] == chosen[:, None, :]) & (order[None, :] < order[:, None])
    rank = jnp.sum(same.astype(jnp.int32), axis=2)
    dx = (chosen // 32 - me // 32) % 2
    dy = (chosen // 8 - me // 8) % 4
    dz = (chosen - me) % 8
    slot = (dx * 32 + dy * 8 + dz) * SLOTS + rank
    held = slot[:, None, :] == jnp.arange(ROWS, dtype=jnp.int32)[None, :, None]
    token = TOK + jnp.sum(jnp.where(held, order // 2 - TOK, 0), axis=2)
    gates = gate_weights[:, 0].reshape(TICKS, 1, -1).astype(jnp.float32)
    gate = jnp.sum(jnp.where(held, gates, 0.0), axis=2)
    slot = slot.reshape(TICKS, TOK, 2).transpose(0, 2, 1)

    smem = pl.BlockSpec(memory_space=pltpu.SMEM)
    vmem = pl.BlockSpec(memory_space=pltpu.VMEM)
    hbm = pl.BlockSpec(memory_space=pl.ANY)
    tiles = pltpu.VMEM((TICKS, ROWS, TILES, LANES), jnp.bfloat16)
    out = pl.pallas_call(
        kernel,
        out_shape=jax.ShapeDtypeStruct((TICKS, TOK, D), jnp.bfloat16),
        in_specs=[smem] * 3 + [vmem] * 4 + [hbm] * 3,
        out_specs=vmem,
        scratch_shapes=[
            pltpu.VMEM((D, FFE), jnp.bfloat16),
            pltpu.VMEM((D, FFE), jnp.bfloat16),
            pltpu.VMEM((FFE, D), jnp.bfloat16),
            tiles, tiles, tiles, tiles, tiles, tiles,
            pltpu.VMEM(((TOK + 1) * TILES, LANES), jnp.float32),
            pltpu.VMEM((GROUP_ROWS * TILES, LANES), jnp.float32),
            pltpu.VMEM((GROUP_ROWS, D), jnp.bfloat16),
            pltpu.VMEM((GROUP_ROWS, D), jnp.bfloat16),
            pltpu.VMEM((TICKS, TOK, LANES), jnp.float32),
            pltpu.VMEM((TOK, D), jnp.bfloat16),
            pltpu.VMEM((TOK, D), jnp.bfloat16),
            pltpu.SemaphoreType.DMA((3,)),
            pltpu.SemaphoreType.DMA((3, TICKS)),
            pltpu.SemaphoreType.DMA((TICKS, GROUPS)),
            pltpu.SemaphoreType.DMA((TICKS, GROUPS)),
            pltpu.SemaphoreType.DMA((TICKS,)),
            pltpu.SemaphoreType.DMA((RELAY,)),
            pltpu.SemaphoreType.DMA((RELAY,)),
        ],
        compiler_params=pltpu.CompilerParams(
            collective_id=0, has_side_effects=True, vmem_limit_bytes=56 << 20
        ),
    )(token, gate, slot, layer_input[:, 0], entering[0], fresh[0], norm_gain, w_gate[0, 0], w_up[0, 0], w_down[0, 0])
    return out[:, None]


def solution(mesh):
    in_specs = (
        P(None, "section", "expert", None),
        P("section", "expert", None),
        P(None, "expert", None),
        P(None, "section", "expert", None),
        P(None, "section", "expert", None),
        P("section", None),
        P("section", "expert", None, None),
        P("section", "expert", None, None),
        P("section", "expert", None, None),
    )
    out_specs = P(None, "section", "expert", None)
    return jax.shard_map(local, mesh=mesh, in_specs=in_specs, out_specs=out_specs, check_vma=False)
```

```python
import functools

import jax
import jax.numpy as jnp
from jax import lax
from jax.experimental import pallas as pl
from jax.experimental.pallas import tpu as pltpu
from jax.sharding import PartitionSpec as P

D = 2048
FFE = 768
TICKS = 2
TOK = 128
PEERS = 64
SLOTS = 6
ROWS = PEERS * SLOTS
GROUPS = 8
IN_GROUP = PEERS // GROUPS
GROUP_ROWS = IN_GROUP * SLOTS
LANES = 128
TILES = D // LANES
RELAY = 4
RELAY_ROWS = TOK // RELAY
UNROLL = 8
MESH = pl.DeviceIdType.MESH

OWN, BEHIND, AHEAD = range(3)
SHIFT = (0, 1, -1)


def peer(me, i, sign):
    dx, dy, dz = i // 32, (i // 8) % 4, i % 8
    x, y, z = me // 32, (me // 8) % 4, me % 8
    return ((x + dx) % 2) * 32 + ((y + sign * dy + 4) % 4) * 8 + (z + sign * dz + 8) % 8


def lanes(c):
    return slice(c * LANES, (c + 1) * LANES)


def contract_last(left, right):
    return lax.dot_general(
        left, right, (((1,), (1,)), ((), ())), preferred_element_type=jnp.float32
    )


def kernel(
    tok_ref, gate_ref, slot_ref, x_ref, entering_ref, fresh_ref, gain_ref, wg_hbm, wu_hbm, wd_hbm,
    out_ref,
    wg, wu, wd, send_a, send_b, send_c, recv_a, recv_b, recv_c, blocks_a, blocks_b, toks, gates,
    by_token, by_slot, rows_a, rows_b, inverse_ref, current, arrived,
    w_sem, send_sem, recv_a_sem, recv_b_sem, recv_c_sem, relay_send_sem, relay_recv_sem,
    block_send_sem, block_recv_sem, table_send_sem, table_recv_sem,
):
    me = lax.axis_index("expert")
    section = lax.axis_index("section")
    last = lax.axis_size("section") - 1

    barrier = pltpu.get_barrier_semaphore()

    def greet(i, carry):
        pl.semaphore_signal(
            barrier, inc=1, device_id=(section, peer(me, i, 1)), device_id_type=MESH
        )
        return carry

    lax.fori_loop(1, PEERS, greet, 0)

    @pl.when(section < last)
    def _():
        pl.semaphore_signal(barrier, inc=1, device_id=(section + 1, me), device_id_type=MESH)

    weight_copies = [
        pltpu.make_async_copy(src, dst, w_sem.at[n])
        for n, (src, dst) in enumerate(((wg_hbm, wg), (wu_hbm, wu), (wd_hbm, wd)))
    ]
    for copy in weight_copies:
        copy.start()

    toks = (tok_ref, *toks)
    gates = (gate_ref, *gates)
    for tick_blocks in (*blocks_a, *blocks_b):
        for block in tick_blocks:
            block[TOK] = jnp.zeros((TILES, LANES), jnp.bfloat16)

    def store_block(block):
        for part in range(RELAY):
            rows = by_token[pl.ds(part * RELAY_ROWS * TILES, RELAY_ROWS * TILES), :]
            block[pl.ds(part * RELAY_ROWS, RELAY_ROWS)] = rows.reshape(RELAY_ROWS, TILES, LANES).astype(jnp.bfloat16)

    def load_normed(tick):
        total = jnp.zeros((TOK, LANES), jnp.float32)
        for c in range(TILES):
            x = x_ref[tick, :, lanes(c)].astype(jnp.float32)
            total = total + x * x
        inverse = lax.rsqrt(jnp.sum(total, axis=1, keepdims=True) / D + 1e-05)
        inverse_ref[tick] = jnp.broadcast_to(inverse, (TOK, LANES))
        for c in range(TILES):
            x = x_ref[tick, :, lanes(c)].astype(jnp.float32)
            by_token[pl.ds(c, TOK, stride=TILES), :] = x * inverse * gain_ref[:, lanes(c)]
        store_block(blocks_a[tick][OWN])

    def load_current(tick):
        for c in range(TILES):
            by_token[pl.ds(c, TOK, stride=TILES), :] = current[:, lanes(c)].astype(jnp.float32)
        store_block(blocks_b[tick][OWN])

    def along_z(src, dst, s_sem, r_sem, step):
        return pltpu.make_async_remote_copy(
            src_ref=src, dst_ref=dst, send_sem=s_sem, recv_sem=r_sem,
            device_id=(section, peer(me, 1, step)), device_id_type=MESH,
        )

    def block_copies(kind, tick):
        blocks = (blocks_a, blocks_b)[kind][tick]
        whole = pl.ds(0, TOK)
        return [
            along_z(
                blocks[OWN].at[whole], blocks[side].at[whole],
                block_send_sem.at[kind, tick, side - 1], block_recv_sem.at[kind, tick, side - 1], SHIFT[side],
            )
            for side in (BEHIND, AHEAD)
        ]

    table_copies = [
        along_z(
            table[OWN], table[side],
            table_send_sem.at[n, side - 1], table_recv_sem.at[n, side - 1], SHIFT[side],
        )
        for n, table in enumerate((toks, gates))
        for side in (BEHIND, AHEAD)
    ]

    def start(copies):
        for copy in copies:
            copy.start()

    def await_arrival(copies):
        for copy in copies:
            copy.wait_recv()

    def stay(src, dst, r_sem, i):
        part = pl.ds(i * SLOTS, SLOTS)
        pltpu.make_async_copy(src.at[part], dst.at[part], r_sem).start()

    def send(src, dst, s_sem, r_sem, i, device):
        part = pl.ds(i * SLOTS, SLOTS)
        pltpu.make_async_remote_copy(
            src_ref=src.at[part], dst_ref=dst.at[part], send_sem=s_sem, recv_sem=r_sem,
            device_id=(section, device), device_id_type=MESH,
        ).start()

    def pack(kind, tick, side, q, dz):
        i = q * 8 + dz
        for r in range(SLOTS):
            s = i * SLOTS + r
            if kind == 0:
                send_a[tick, s] = blocks_a[tick][side][toks[side][tick, s]]
            else:
                rows = blocks_b[tick][side][toks[side][tick, s]].astype(jnp.float32)
                send_b[tick, s] = (rows * gates[side][tick, s]).astype(jnp.bfloat16)
        src, dst = ((send_a, recv_a), (send_b, recv_b))[kind]
        src, dst, s_sem = src.at[tick], dst.at[tick], send_sem.at[kind, tick]
        r_sem = (recv_a_sem, recv_b_sem)[kind].at[tick, q]
        left = (dz - SHIFT[side]) % 8
        if left != 0:
            send(src, dst, s_sem, r_sem, i, peer(me, q * 8 + left, 1))
            return

        @pl.when(q == 0)
        def _():
            stay(src, dst, r_sem, i)

        @pl.when(q > 0)
        def _():
            send(src, dst, s_sem, r_sem, i, peer(me, q * 8, 1))

    def pack_own(kind, tick):
        def body(q, carry):
            pack(kind, tick, OWN, q, 0)
            return carry

        lax.fori_loop(0, GROUPS, body, 0)

    def pack_sides(kind, tick):
        def body(half, carry):
            for odd in range(2):
                q = half * 2 + odd
                for dz in range(1, 4):
                    pack(kind, tick, BEHIND, q, dz)
                    pack(kind, tick, AHEAD, q, 8 - dz)
                pack(kind, tick, (BEHIND, AHEAD)[odd], q, 4)
            return carry

        lax.fori_loop(0, GROUPS // 2, body, 0)

    def wait_bytes(ref, sem):
        pltpu.make_async_copy(ref, ref, sem).wait()

    def to_rows(tiles, rows):
        by_slot[...] = tiles.astype(jnp.float32).reshape(GROUP_ROWS * TILES, LANES)
        for c in range(TILES):
            rows[:, lanes(c)] = by_slot[pl.ds(c, GROUP_ROWS, stride=TILES), :].astype(jnp.bfloat16)

    def experts(tick):
        def body(g, carry):
            part = pl.ds(g * GROUP_ROWS, GROUP_ROWS)
            wait_bytes(recv_a.at[tick, part], recv_a_sem.at[tick, g])
            wait_bytes(recv_b.at[tick, part], recv_b_sem.at[tick, g])
            to_rows(recv_a[tick, part], rows_a)
            to_rows(recv_b[tick, part], rows_b)
            normed = rows_a[...]
            pre_gate = jnp.dot(normed, wg[...], preferred_element_type=jnp.float32)
            pre_up = jnp.dot(normed, wu[...], preferred_element_type=jnp.float32)
            hidden_grad = contract_last(rows_b[...], wd[...])
            sigmoid = jax.nn.sigmoid(pre_gate)
            gate_grad = (
                hidden_grad * pre_up * sigmoid * (1.0 + pre_gate * (1.0 - sigmoid))
            ).astype(jnp.bfloat16)
            up_grad = (hidden_grad * pre_gate * sigmoid).astype(jnp.bfloat16)
            summed = contract_last(gate_grad, wg[...]) + contract_last(up_grad, wu[...])
            for c in range(TILES):
                by_slot[pl.ds(c, GROUP_ROWS, stride=TILES), :] = summed[:, lanes(c)]
            send_c[tick, part] = by_slot[...].reshape(GROUP_ROWS, TILES, LANES).astype(jnp.bfloat16)

            def give_back(j, inner):
                i = g * IN_GROUP + j

                @pl.when(i == 0)
                def _():
                    stay(send_c.at[tick], recv_c.at[tick], recv_c_sem.at[tick], i)

                @pl.when(i > 0)
                def _():
                    send(
                        send_c.at[tick], recv_c.at[tick], send_sem.at[2, tick], recv_c_sem.at[tick],
                        i, peer(me, i, -1),
                    )

                return inner

            lax.fori_loop(0, IN_GROUP, give_back, 0)
            return carry

        lax.fori_loop(0, GROUPS, body, 0)

    def combine(tick):
        wait_bytes(recv_c.at[tick], recv_c_sem.at[tick])

        def add(n, carry):
            for u in range(UNROLL):
                t = n * UNROLL + u
                by_token[pl.ds(pl.multiple_of(t * TILES, TILES), TILES), :] = recv_c[
                    tick, slot_ref[tick, 0, t]
                ].astype(jnp.float32) + recv_c[tick, slot_ref[tick, 1, t]].astype(jnp.float32)
            return carry

        lax.fori_loop(0, TOK // UNROLL, add, 0)
        for part in range(RELAY):
            first = part * RELAY_ROWS
            rows = slice(first, first + RELAY_ROWS)
            total = jnp.zeros((RELAY_ROWS, LANES), jnp.float32)
            for c in range(TILES):
                weighted = gain_ref[:, lanes(c)] * by_token[pl.ds(first * TILES + c, RELAY_ROWS, stride=TILES), :]
                total = total + x_ref[tick, rows, lanes(c)].astype(jnp.float32) * weighted
            project = jnp.sum(total, axis=1, keepdims=True) / D
            inverse = inverse_ref[tick, rows]
            cubed = inverse * inverse * inverse * project
            for c in range(TILES):
                weighted = gain_ref[:, lanes(c)] * by_token[pl.ds(first * TILES + c, RELAY_ROWS, stride=TILES), :]
                out_ref[tick, rows, lanes(c)] = (
                    current[rows, lanes(c)].astype(jnp.float32)
                    + inverse * weighted
                    - x_ref[tick, rows, lanes(c)].astype(jnp.float32) * cubed
                ).astype(jnp.bfloat16)
            if tick == 0:

                @pl.when(section > 0)
                def _():
                    relay(part).start()

    def relay(part):
        rows = pl.ds(part * RELAY_ROWS, RELAY_ROWS)
        return pltpu.make_async_remote_copy(
            src_ref=out_ref.at[0, rows],
            dst_ref=arrived.at[rows],
            send_sem=relay_send_sem.at[part],
            recv_sem=relay_recv_sem.at[part],
            device_id=(section - 1, me),
            device_id_type=MESH,
        )

    current[...] = entering_ref[...]
    load_current(0)

    @pl.when(section == 0)
    def _():
        pl.semaphore_wait(barrier, PEERS - 1)

    @pl.when(section > 0)
    def _():
        pl.semaphore_wait(barrier, PEERS)

    start(table_copies)
    start(block_copies(1, 0))
    load_normed(0)
    start(block_copies(0, 0))
    pack_own(1, 0)
    pack_own(0, 0)
    load_normed(1)
    await_arrival(table_copies)
    await_arrival(block_copies(1, 0))
    pack_sides(1, 0)
    await_arrival(block_copies(0, 0))
    pack_sides(0, 0)
    for copy in weight_copies:
        copy.wait()
    experts(0)
    start(block_copies(0, 1))
    pack_own(0, 1)
    combine(0)

    @pl.when(section < last)
    def _():
        for part in range(RELAY):
            rows = pl.ds(part * RELAY_ROWS, RELAY_ROWS)
            wait_bytes(arrived.at[rows], relay_recv_sem.at[part])
        current[...] = arrived[...]

    @pl.when(section == last)
    def _():
        current[...] = fresh_ref[...]

    load_current(1)
    start(block_copies(1, 1))
    pack_own(1, 1)
    await_arrival(block_copies(0, 1))
    pack_sides(0, 1)
    await_arrival(block_copies(1, 1))
    pack_sides(1, 1)
    experts(1)
    combine(1)

    @pl.when(section > 0)
    def _():
        for part in range(RELAY):
            relay(part).wait_send()

    for copy in table_copies:
        copy.wait_send()
    for kind in range(2):
        for tick in range(TICKS):
            for copy in block_copies(kind, tick):
                copy.wait_send()
    for kind, (sent, stayed) in enumerate(((send_a, 3), (send_b, 3), (send_c, 1))):
        for tick in range(TICKS):
            wait_bytes(sent.at[tick, pl.ds(stayed * SLOTS, ROWS - stayed * SLOTS)], send_sem.at[kind, tick])


def local(layer_input, entering, fresh, routes, gate_weights, norm_gain, w_gate, w_up, w_down):
    me = lax.axis_index("expert")
    chosen = routes[:, 0].reshape(TICKS, -1)
    order = jnp.arange(2 * TOK, dtype=jnp.int32)
    same = (chosen[:, :, None] == chosen[:, None, :]) & (order[None, :] < order[:, None])
    rank = jnp.sum(same.astype(jnp.int32), axis=2)
    dx = (chosen // 32 - me // 32) % 2
    dy = (chosen // 8 - me // 8) % 4
    dz = (chosen - me) % 8
    slot = (dx * 32 + dy * 8 + dz) * SLOTS + rank
    held = slot[:, None, :] == jnp.arange(ROWS, dtype=jnp.int32)[None, :, None]
    token = TOK + jnp.sum(jnp.where(held, order // 2 - TOK, 0), axis=2)
    gates = gate_weights[:, 0].reshape(TICKS, 1, -1).astype(jnp.float32)
    gate = jnp.sum(jnp.where(held, gates, 0.0), axis=2)
    slot = slot.reshape(TICKS, TOK, 2).transpose(0, 2, 1)

    smem = pl.BlockSpec(memory_space=pltpu.SMEM)
    vmem = pl.BlockSpec(memory_space=pltpu.VMEM)
    hbm = pl.BlockSpec(memory_space=pl.ANY)
    tiles = pltpu.VMEM((TICKS, ROWS, TILES, LANES), jnp.bfloat16)
    blocks = [[pltpu.VMEM((TOK + 1, TILES, LANES), jnp.bfloat16)] * 3] * TICKS
    out = pl.pallas_call(
        kernel,
        out_shape=jax.ShapeDtypeStruct((TICKS, TOK, D), jnp.bfloat16),
        in_specs=[smem] * 3 + [vmem] * 4 + [hbm] * 3,
        out_specs=vmem,
        scratch_shapes=[
            pltpu.VMEM((D, FFE), jnp.bfloat16),
            pltpu.VMEM((D, FFE), jnp.bfloat16),
            pltpu.VMEM((FFE, D), jnp.bfloat16),
            tiles, tiles, tiles, tiles, tiles, tiles,
            blocks, blocks,
            [pltpu.SMEM((TICKS, ROWS), jnp.int32)] * 2,
            [pltpu.SMEM((TICKS, ROWS), jnp.float32)] * 2,
            pltpu.VMEM((TOK * TILES, LANES), jnp.float32),
            pltpu.VMEM((GROUP_ROWS * TILES, LANES), jnp.float32),
            pltpu.VMEM((GROUP_ROWS, D), jnp.bfloat16),
            pltpu.VMEM((GROUP_ROWS, D), jnp.bfloat16),
            pltpu.VMEM((TICKS, TOK, LANES), jnp.float32),
            pltpu.VMEM((TOK, D), jnp.bfloat16),
            pltpu.VMEM((TOK, D), jnp.bfloat16),
            pltpu.SemaphoreType.DMA((3,)),
            pltpu.SemaphoreType.DMA((3, TICKS)),
            pltpu.SemaphoreType.DMA((TICKS, GROUPS)),
            pltpu.SemaphoreType.DMA((TICKS, GROUPS)),
            pltpu.SemaphoreType.DMA((TICKS,)),
            pltpu.SemaphoreType.DMA((RELAY,)),
            pltpu.SemaphoreType.DMA((RELAY,)),
            pltpu.SemaphoreType.DMA((2, TICKS, 2)),
            pltpu.SemaphoreType.DMA((2, TICKS, 2)),
            pltpu.SemaphoreType.DMA((2, 2)),
            pltpu.SemaphoreType.DMA((2, 2)),
        ],
        compiler_params=pltpu.CompilerParams(
            collective_id=0, has_side_effects=True, vmem_limit_bytes=56 << 20
        ),
    )(token, gate, slot, layer_input[:, 0], entering[0], fresh[0], norm_gain, w_gate[0, 0], w_up[0, 0], w_down[0, 0])
    return out[:, None]


def solution(mesh):
    in_specs = (
        P(None, "section", "expert", None),
        P("section", "expert", None),
        P(None, "expert", None),
        P(None, "section", "expert", None),
        P(None, "section", "expert", None),
        P("section", None),
        P("section", "expert", None, None),
        P("section", "expert", None, None),
        P("section", "expert", None, None),
    )
    out_specs = P(None, "section", "expert", None)
    return jax.shard_map(local, mesh=mesh, in_specs=in_specs, out_specs=out_specs, check_vma=False)
```

```python
import functools

import jax
import jax.numpy as jnp
from jax import lax
from jax.experimental import pallas as pl
from jax.experimental.pallas import tpu as pltpu
from jax.sharding import PartitionSpec as P

D = 2048
FFE = 768
TICKS = 2
TOK = 128
PEERS = 64
SLOTS = 6
ROWS = PEERS * SLOTS
GROUPS = 8
IN_GROUP = PEERS // GROUPS
GROUP_ROWS = IN_GROUP * SLOTS
LANES = 128
TILES = D // LANES
RELAY = 4
RELAY_ROWS = TOK // RELAY
UNROLL = 8
MESH = pl.DeviceIdType.MESH

OWN, BEHIND, AHEAD = range(3)
SHIFT = (0, 1, -1)


def peer(me, i, sign):
    dx, dy, dz = i // 32, (i // 8) % 4, i % 8
    x, y, z = me // 32, (me // 8) % 4, me % 8
    return ((x + dx) % 2) * 32 + ((y + sign * dy + 4) % 4) * 8 + (z + sign * dz + 8) % 8


def lanes(c):
    return slice(c * LANES, (c + 1) * LANES)


def contract_last(left, right):
    return lax.dot_general(
        left, right, (((1,), (1,)), ((), ())), preferred_element_type=jnp.float32
    )


def kernel(
    routes_ref, gates_ref, x_ref, entering_ref, fresh_ref, gain_ref, wg_hbm, wu_hbm, wd_hbm,
    out_ref,
    wg, wu, wd, send_a, send_b, send_c, recv_a, recv_b, recv_c, blocks_a, blocks_b, toks, gates, slot_ref,
    tok_made, gate_made, slot_made,
    by_token, by_slot, rows_a, rows_b, inverse_ref, current, arrived,
    w_sem, send_sem, recv_a_sem, recv_b_sem, recv_c_sem, relay_send_sem, relay_recv_sem,
    block_send_sem, block_recv_sem, table_send_sem, table_recv_sem, made_sem, greet_sem,
):
    me = lax.axis_index("expert")
    section = lax.axis_index("section")
    last = lax.axis_size("section") - 1

    barrier = pltpu.get_barrier_semaphore()

    def greet(sem, i):
        pl.semaphore_signal(sem, inc=1, device_id=(section, peer(me, i, 1)), device_id_type=MESH)

    ring_z, ring_y, ring_x = range(1, 8), (8, 16, 24), (32,)
    for i in (*ring_z, *ring_y, *ring_x):
        greet(barrier, i)

    @pl.when(section < last)
    def _():
        pl.semaphore_signal(barrier, inc=1, device_id=(section + 1, me), device_id_type=MESH)

    weight_copies = [
        pltpu.make_async_copy(src, dst, w_sem.at[n])
        for n, (src, dst) in enumerate(((wg_hbm, wg), (wu_hbm, wu), (wd_hbm, wd)))
    ]
    for copy in weight_copies:
        copy.start()

    for tick_blocks in (*blocks_a, *blocks_b):
        for block in tick_blocks:
            block[TOK] = jnp.zeros((TILES, LANES), jnp.bfloat16)

    def store_block(block):
        for part in range(RELAY):
            rows = by_token[pl.ds(part * RELAY_ROWS * TILES, RELAY_ROWS * TILES), :]
            block[pl.ds(part * RELAY_ROWS, RELAY_ROWS)] = rows.reshape(RELAY_ROWS, TILES, LANES).astype(jnp.bfloat16)

    def load_normed(tick):
        total = jnp.zeros((TOK, LANES), jnp.float32)
        for c in range(TILES):
            x = x_ref[tick, :, lanes(c)].astype(jnp.float32)
            total = total + x * x
        inverse = lax.rsqrt(jnp.sum(total, axis=1, keepdims=True) / D + 1e-05)
        inverse_ref[tick] = jnp.broadcast_to(inverse, (TOK, LANES))
        for c in range(TILES):
            x = x_ref[tick, :, lanes(c)].astype(jnp.float32)
            by_token[pl.ds(c, TOK, stride=TILES), :] = x * inverse * gain_ref[:, lanes(c)]
        store_block(blocks_a[tick][OWN])

    def load_current(tick):
        for c in range(TILES):
            by_token[pl.ds(c, TOK, stride=TILES), :] = current[:, lanes(c)].astype(jnp.float32)
        store_block(blocks_b[tick][OWN])

    def along_z(src, dst, s_sem, r_sem, step):
        return pltpu.make_async_remote_copy(
            src_ref=src, dst_ref=dst, send_sem=s_sem, recv_sem=r_sem,
            device_id=(section, peer(me, 1, step)), device_id_type=MESH,
        )

    def block_copies(kind, tick):
        blocks = (blocks_a, blocks_b)[kind][tick]
        whole = pl.ds(0, TOK)
        return [
            along_z(
                blocks[OWN].at[whole], blocks[side].at[whole],
                block_send_sem.at[kind, tick, side - 1], block_recv_sem.at[kind, tick, side - 1], SHIFT[side],
            )
            for side in (BEHIND, AHEAD)
        ]

    table_copies = [
        along_z(
            table[OWN], table[side],
            table_send_sem.at[n, side - 1], table_recv_sem.at[n, side - 1], SHIFT[side],
        )
        for n, table in enumerate((toks, gates))
        for side in (BEHIND, AHEAD)
    ]

    def start(copies):
        for copy in copies:
            copy.start()

    def await_arrival(copies):
        for copy in copies:
            copy.wait_recv()

    def stay(src, dst, r_sem, i):
        part = pl.ds(i * SLOTS, SLOTS)
        pltpu.make_async_copy(src.at[part], dst.at[part], r_sem).start()

    def send(src, dst, s_sem, r_sem, i, device):
        part = pl.ds(i * SLOTS, SLOTS)
        pltpu.make_async_remote_copy(
            src_ref=src.at[part], dst_ref=dst.at[part], send_sem=s_sem, recv_sem=r_sem,
            device_id=(section, device), device_id_type=MESH,
        ).start()

    def pack(kind, tick, side, q, dz):
        i = q * 8 + dz
        for r in range(SLOTS):
            s = i * SLOTS + r
            if kind == 0:
                send_a[tick, s] = blocks_a[tick][side][toks[side][tick, s]]
            else:
                rows = blocks_b[tick][side][toks[side][tick, s]].astype(jnp.float32)
                send_b[tick, s] = (rows * gates[side][tick, s]).astype(jnp.bfloat16)
        src, dst = ((send_a, recv_a), (send_b, recv_b))[kind]
        src, dst, s_sem = src.at[tick], dst.at[tick], send_sem.at[kind, tick]
        r_sem = (recv_a_sem, recv_b_sem)[kind].at[tick, q]
        left = (dz - SHIFT[side]) % 8
        if left != 0:
            send(src, dst, s_sem, r_sem, i, peer(me, q * 8 + left, 1))
            return

        @pl.when(q == 0)
        def _():
            stay(src, dst, r_sem, i)

        @pl.when(q > 0)
        def _():
            send(src, dst, s_sem, r_sem, i, peer(me, q * 8, 1))

    def pack_own(kind, tick):
        def body(q, carry):
            pack(kind, tick, OWN, q, 0)
            return carry

        lax.fori_loop(0, GROUPS, body, 0)

    def pack_sides(kind, tick, first=0, end=GROUPS // 2):
        def body(half, carry):
            for odd in range(2):
                q = half * 2 + odd
                for dz in range(1, 4):
                    pack(kind, tick, BEHIND, q, dz)
                    pack(kind, tick, AHEAD, q, 8 - dz)
                pack(kind, tick, (BEHIND, AHEAD)[odd], q, 4)
            return carry

        lax.fori_loop(first, end, body, 0)

    def wait_bytes(ref, sem):
        pltpu.make_async_copy(ref, ref, sem).wait()

    def to_rows(tiles, rows):
        by_slot[...] = tiles.astype(jnp.float32).reshape(GROUP_ROWS * TILES, LANES)
        for c in range(TILES):
            rows[:, lanes(c)] = by_slot[pl.ds(c, GROUP_ROWS, stride=TILES), :].astype(jnp.bfloat16)

    def experts(tick):
        def body(g, carry):
            part = pl.ds(g * GROUP_ROWS, GROUP_ROWS)
            wait_bytes(recv_a.at[tick, part], recv_a_sem.at[tick, g])
            wait_bytes(recv_b.at[tick, part], recv_b_sem.at[tick, g])
            to_rows(recv_a[tick, part], rows_a)
            to_rows(recv_b[tick, part], rows_b)
            normed = rows_a[...]
            pre_gate = jnp.dot(normed, wg[...], preferred_element_type=jnp.float32)
            pre_up = jnp.dot(normed, wu[...], preferred_element_type=jnp.float32)
            hidden_grad = contract_last(rows_b[...], wd[...])
            sigmoid = jax.nn.sigmoid(pre_gate)
            gate_grad = (
                hidden_grad * pre_up * sigmoid * (1.0 + pre_gate * (1.0 - sigmoid))
            ).astype(jnp.bfloat16)
            up_grad = (hidden_grad * pre_gate * sigmoid).astype(jnp.bfloat16)
            summed = contract_last(gate_grad, wg[...]) + contract_last(up_grad, wu[...])
            for c in range(TILES):
                by_slot[pl.ds(c, GROUP_ROWS, stride=TILES), :] = summed[:, lanes(c)]
            send_c[tick, part] = by_slot[...].reshape(GROUP_ROWS, TILES, LANES).astype(jnp.bfloat16)

            def give_back(j, inner):
                i = g * IN_GROUP + j

                @pl.when(i == 0)
                def _():
                    stay(send_c.at[tick], recv_c.at[tick], recv_c_sem.at[tick], i)

                @pl.when(i > 0)
                def _():
                    send(
                        send_c.at[tick], recv_c.at[tick], send_sem.at[2, tick], recv_c_sem.at[tick],
                        i, peer(me, i, -1),
                    )

                return inner

            lax.fori_loop(0, IN_GROUP, give_back, 0)
            return carry

        lax.fori_loop(0, GROUPS, body, 0)

    def combine(tick):
        wait_bytes(recv_c.at[tick], recv_c_sem.at[tick])

        def add(n, carry):
            for u in range(UNROLL):
                t = n * UNROLL + u
                by_token[pl.ds(pl.multiple_of(t * TILES, TILES), TILES), :] = recv_c[
                    tick, slot_ref[tick, 0, t]
                ].astype(jnp.float32) + recv_c[tick, slot_ref[tick, 1, t]].astype(jnp.float32)
            return carry

        lax.fori_loop(0, TOK // UNROLL, add, 0)
        for part in range(RELAY):
            first = part * RELAY_ROWS
            rows = slice(first, first + RELAY_ROWS)
            total = jnp.zeros((RELAY_ROWS, LANES), jnp.float32)
            for c in range(TILES):
                weighted = gain_ref[:, lanes(c)] * by_token[pl.ds(first * TILES + c, RELAY_ROWS, stride=TILES), :]
                total = total + x_ref[tick, rows, lanes(c)].astype(jnp.float32) * weighted
            project = jnp.sum(total, axis=1, keepdims=True) / D
            inverse = inverse_ref[tick, rows]
            cubed = inverse * inverse * inverse * project
            for c in range(TILES):
                weighted = gain_ref[:, lanes(c)] * by_token[pl.ds(first * TILES + c, RELAY_ROWS, stride=TILES), :]
                out_ref[tick, rows, lanes(c)] = (
                    current[rows, lanes(c)].astype(jnp.float32)
                    + inverse * weighted
                    - x_ref[tick, rows, lanes(c)].astype(jnp.float32) * cubed
                ).astype(jnp.bfloat16)
            if tick == 0:

                @pl.when(section > 0)
                def _():
                    relay(part).start()

    def relay(part):
        rows = pl.ds(part * RELAY_ROWS, RELAY_ROWS)
        return pltpu.make_async_remote_copy(
            src_ref=out_ref.at[0, rows],
            dst_ref=arrived.at[rows],
            send_sem=relay_send_sem.at[part],
            recv_sem=relay_recv_sem.at[part],
            device_id=(section - 1, me),
            device_id_type=MESH,
        )

    def make_tables():
        down = lax.broadcasted_iota(jnp.int32, (TOK, TOK), 0)
        across = lax.broadcasted_iota(jnp.int32, (TOK, TOK), 1)
        slot_at = lax.broadcasted_iota(jnp.int32, (TOK, ROWS), 1)
        token_less = lax.broadcasted_iota(jnp.int32, (TOK, ROWS), 0) - TOK

        def column(row):
            return jnp.sum(jnp.where(down == across, row, jnp.zeros_like(row)), axis=1, keepdims=True)

        x, y, z = me // 32, (me // 8) % 4, me % 8
        for tick in range(TICKS):
            chosen = [routes_ref[tick, k : k + 1, :] for k in range(2)]
            columns = [column(row) for row in chosen]
            token = jnp.zeros((1, ROWS), jnp.int32)
            gate = jnp.zeros((1, ROWS), jnp.float32)
            for k in range(2):
                rank = jnp.zeros((1, TOK), jnp.int32)
                for other in columns:
                    same = (other == chosen[k]) & (down < across)
                    rank = rank + jnp.sum(jnp.where(same, 1, 0), axis=0, keepdims=True)
                dx = ((chosen[k] >> 5) - x) & 1
                dy = ((chosen[k] >> 3) - y) & 3
                dz = (chosen[k] - z) & 7
                slot = ((dx << 5) + (dy << 3) + dz) * SLOTS + rank
                slot_made[tick, k : k + 1, :] = jnp.minimum(slot, ROWS - 1)
                held = column(slot) == slot_at
                gate_column = column(gates_ref[tick, k : k + 1, :].astype(jnp.float32))
                token = token + jnp.sum(jnp.where(held, token_less, 0), axis=0, keepdims=True)
                gate = gate + jnp.sum(jnp.where(held, gate_column, 0.0), axis=0, keepdims=True)
            tok_made[tick : tick + 1, :] = jnp.clip(token + TOK, 0, TOK)
            gate_made[tick : tick + 1, :] = gate

    current[...] = entering_ref[...]
    load_current(0)

    @pl.when(section == 0)
    def _():
        pl.semaphore_wait(barrier, 11)

    @pl.when(section > 0)
    def _():
        pl.semaphore_wait(barrier, 12)

    for i in ring_y:
        greet(greet_sem.at[0], i)
    start(block_copies(1, 0))
    load_normed(0)
    start(block_copies(0, 0))
    make_tables()
    made_copies = [
        pltpu.make_async_copy(made, held, made_sem.at[n])
        for n, (made, held) in enumerate(((tok_made, toks[OWN]), (gate_made, gates[OWN]), (slot_made, slot_ref)))
    ]
    start(made_copies)
    pl.semaphore_wait(greet_sem.at[0], 3)
    for i in ring_x:
        greet(greet_sem.at[1], i)
    for copy in made_copies:
        copy.wait()
    start(table_copies)
    load_normed(1)
    start(block_copies(0, 1))
    pl.semaphore_wait(greet_sem.at[1], 1)
    pack_own(1, 0)
    pack_own(0, 0)
    await_arrival(table_copies)
    await_arrival(block_copies(1, 0))
    pack_sides(1, 0)
    await_arrival(block_copies(0, 0))
    pack_sides(0, 0)
    for copy in weight_copies:
        copy.wait()
    experts(0)
    pack_own(0, 1)
    await_arrival(block_copies(0, 1))
    pack_sides(0, 1, 0, 2)
    combine(0)

    @pl.when(section < last)
    def _():
        for part in range(RELAY):
            rows = pl.ds(part * RELAY_ROWS, RELAY_ROWS)
            wait_bytes(arrived.at[rows], relay_recv_sem.at[part])
        current[...] = arrived[...]

    @pl.when(section == last)
    def _():
        current[...] = fresh_ref[...]

    load_current(1)
    start(block_copies(1, 1))
    pack_own(1, 1)
    pack_sides(0, 1, 2, 4)
    await_arrival(block_copies(1, 1))
    pack_sides(1, 1)
    experts(1)
    combine(1)

    @pl.when(section > 0)
    def _():
        for part in range(RELAY):
            relay(part).wait_send()

    for copy in table_copies:
        copy.wait_send()
    for kind in range(2):
        for tick in range(TICKS):
            for copy in block_copies(kind, tick):
                copy.wait_send()
    for kind, (sent, stayed) in enumerate(((send_a, 3), (send_b, 3), (send_c, 1))):
        for tick in range(TICKS):
            wait_bytes(sent.at[tick, pl.ds(stayed * SLOTS, ROWS - stayed * SLOTS)], send_sem.at[kind, tick])


def local(layer_input, entering, fresh, routes, gate_weights, norm_gain, w_gate, w_up, w_down):
    by_choice = [a[:, 0].transpose(0, 2, 1) for a in (routes, gate_weights)]
    vmem = pl.BlockSpec(memory_space=pltpu.VMEM)
    hbm = pl.BlockSpec(memory_space=pl.ANY)
    tiles = pltpu.VMEM((TICKS, ROWS, TILES, LANES), jnp.bfloat16)
    blocks = [[pltpu.VMEM((TOK + 1, TILES, LANES), jnp.bfloat16)] * 3] * TICKS
    out = pl.pallas_call(
        kernel,
        out_shape=jax.ShapeDtypeStruct((TICKS, TOK, D), jnp.bfloat16),
        in_specs=[vmem] * 6 + [hbm] * 3,
        out_specs=vmem,
        scratch_shapes=[
            pltpu.VMEM((D, FFE), jnp.bfloat16),
            pltpu.VMEM((D, FFE), jnp.bfloat16),
            pltpu.VMEM((FFE, D), jnp.bfloat16),
            tiles, tiles, tiles, tiles, tiles, tiles,
            blocks, blocks,
            [pltpu.SMEM((TICKS, ROWS), jnp.int32)] * 3,
            [pltpu.SMEM((TICKS, ROWS), jnp.float32)] * 3,
            pltpu.SMEM((TICKS, 2, TOK), jnp.int32),
            pltpu.VMEM((TICKS, ROWS), jnp.int32),
            pltpu.VMEM((TICKS, ROWS), jnp.float32),
            pltpu.VMEM((TICKS, 2, TOK), jnp.int32),
            pltpu.VMEM((TOK * TILES, LANES), jnp.float32),
            pltpu.VMEM((GROUP_ROWS * TILES, LANES), jnp.float32),
            pltpu.VMEM((GROUP_ROWS, D), jnp.bfloat16),
            pltpu.VMEM((GROUP_ROWS, D), jnp.bfloat16),
            pltpu.VMEM((TICKS, TOK, LANES), jnp.float32),
            pltpu.VMEM((TOK, D), jnp.bfloat16),
            pltpu.VMEM((TOK, D), jnp.bfloat16),
            pltpu.SemaphoreType.DMA((3,)),
            pltpu.SemaphoreType.DMA((3, TICKS)),
            pltpu.SemaphoreType.DMA((TICKS, GROUPS)),
            pltpu.SemaphoreType.DMA((TICKS, GROUPS)),
            pltpu.SemaphoreType.DMA((TICKS,)),
            pltpu.SemaphoreType.DMA((RELAY,)),
            pltpu.SemaphoreType.DMA((RELAY,)),
            pltpu.SemaphoreType.DMA((2, TICKS, 2)),
            pltpu.SemaphoreType.DMA((2, TICKS, 2)),
            pltpu.SemaphoreType.DMA((2, 2)),
            pltpu.SemaphoreType.DMA((2, 2)),
            pltpu.SemaphoreType.DMA((3,)),
            pltpu.SemaphoreType.REGULAR((2,)),
        ],
        compiler_params=pltpu.CompilerParams(
            collective_id=0, has_side_effects=True, vmem_limit_bytes=56 << 20
        ),
    )(*by_choice, layer_input[:, 0], entering[0], fresh[0], norm_gain, w_gate[0, 0], w_up[0, 0], w_down[0, 0])
    return out[:, None]


def solution(mesh):
    in_specs = (
        P(None, "section", "expert", None),
        P("section", "expert", None),
        P(None, "expert", None),
        P(None, "section", "expert", None),
        P(None, "section", "expert", None),
        P("section", None),
        P("section", "expert", None, None),
        P("section", "expert", None, None),
        P("section", "expert", None, None),
    )
    out_specs = P(None, "section", "expert", None)
    return jax.shard_map(local, mesh=mesh, in_specs=in_specs, out_specs=out_specs, check_vma=False)
```

```python
import functools

import jax
import jax.numpy as jnp
from jax import lax
from jax.experimental import pallas as pl
from jax.experimental.pallas import tpu as pltpu
from jax.sharding import PartitionSpec as P

D = 2048
FFE = 768
TICKS = 2
TOK = 128
PEERS = 64
SLOTS = 6
ROWS = PEERS * SLOTS
GROUPS = 8
IN_GROUP = PEERS // GROUPS
GROUP_ROWS = IN_GROUP * SLOTS
LANES = 128
TILES = D // LANES
RELAY = 4
RELAY_ROWS = TOK // RELAY
UNROLL = 8
MESH = pl.DeviceIdType.MESH

OWN, BEHIND, AHEAD = range(3)
SHIFT = (0, 1, -1)


def peer(me, i, sign):
    dx, dy, dz = i // 32, (i // 8) % 4, i % 8
    x, y, z = me // 32, (me // 8) % 4, me % 8
    return ((x + dx) % 2) * 32 + ((y + sign * dy + 4) % 4) * 8 + (z + sign * dz + 8) % 8


def lanes(c):
    return slice(c * LANES, (c + 1) * LANES)


def contract_last(left, right):
    return lax.dot_general(
        left, right, (((1,), (1,)), ((), ())), preferred_element_type=jnp.float32
    )


def kernel(
    routes_ref, gates_ref, x_ref, entering_ref, fresh_ref, gain_ref, wg_hbm, wu_hbm, wd_hbm,
    out_ref,
    wg, wu, wd, send_a, send_b, send_c, recv_a, recv_b, recv_c, blocks_a, blocks_b, toks, gates, slot_ref,
    tok_made, gate_made, slot_made,
    by_token, by_slot, rows_a, rows_b, inverse_ref, current, arrived,
    w_sem, send_sem, recv_a_sem, recv_b_sem, recv_c_sem, relay_send_sem, relay_recv_sem,
    block_send_sem, block_recv_sem, table_send_sem, table_recv_sem, made_sem, greet_sem,
):
    me = lax.axis_index("expert")
    section = lax.axis_index("section")
    last = lax.axis_size("section") - 1
    lower = section < 2

    barrier = pltpu.get_barrier_semaphore()

    def greet(sem, i):
        pl.semaphore_signal(sem, inc=1, device_id=(section, peer(me, i, 1)), device_id_type=MESH)

    ring_z, ring_y, ring_x = range(1, 8), (8, 16, 24), (32,)
    for i in (*ring_z, *ring_y, *ring_x):
        greet(barrier, i)

    @pl.when(section < last)
    def _():
        pl.semaphore_signal(barrier, inc=1, device_id=(section + 1, me), device_id_type=MESH)

    weight_copies = [
        pltpu.make_async_copy(src, dst, w_sem.at[n])
        for n, (src, dst) in enumerate(((wg_hbm, wg), (wu_hbm, wu), (wd_hbm, wd)))
    ]
    for copy in weight_copies:
        copy.start()

    for tick_blocks in (*blocks_a, *blocks_b):
        for block in tick_blocks:
            block[TOK] = jnp.zeros((TILES, LANES), jnp.bfloat16)

    def store_block(block):
        for part in range(RELAY):
            rows = by_token[pl.ds(part * RELAY_ROWS * TILES, RELAY_ROWS * TILES), :]
            block[pl.ds(part * RELAY_ROWS, RELAY_ROWS)] = rows.reshape(RELAY_ROWS, TILES, LANES).astype(jnp.bfloat16)

    def load_normed(tick):
        total = jnp.zeros((TOK, LANES), jnp.float32)
        for c in range(TILES):
            x = x_ref[tick, :, lanes(c)].astype(jnp.float32)
            total = total + x * x
        inverse = lax.rsqrt(jnp.sum(total, axis=1, keepdims=True) / D + 1e-05)
        inverse_ref[tick] = jnp.broadcast_to(inverse, (TOK, LANES))
        for c in range(TILES):
            x = x_ref[tick, :, lanes(c)].astype(jnp.float32)
            by_token[pl.ds(c, TOK, stride=TILES), :] = x * inverse * gain_ref[:, lanes(c)]
        store_block(blocks_a[tick][OWN])

    def load_current(tick):
        for c in range(TILES):
            by_token[pl.ds(c, TOK, stride=TILES), :] = current[:, lanes(c)].astype(jnp.float32)
        store_block(blocks_b[tick][OWN])

    def along_z(src, dst, s_sem, r_sem, step):
        return pltpu.make_async_remote_copy(
            src_ref=src, dst_ref=dst, send_sem=s_sem, recv_sem=r_sem,
            device_id=(section, peer(me, 1, step)), device_id_type=MESH,
        )

    def block_copies(kind, tick):
        blocks = (blocks_a, blocks_b)[kind][tick]
        whole = pl.ds(0, TOK)
        return [
            along_z(
                blocks[OWN].at[whole], blocks[side].at[whole],
                block_send_sem.at[kind, tick, side - 1], block_recv_sem.at[kind, tick, side - 1], SHIFT[side],
            )
            for side in (BEHIND, AHEAD)
        ]

    table_copies = [
        along_z(
            table[OWN], table[side],
            table_send_sem.at[n, side - 1], table_recv_sem.at[n, side - 1], SHIFT[side],
        )
        for n, table in enumerate((toks, gates))
        for side in (BEHIND, AHEAD)
    ]

    def start(copies):
        for copy in copies:
            copy.start()

    def await_arrival(copies):
        for copy in copies:
            copy.wait_recv()

    def stay(src, dst, r_sem, i):
        part = pl.ds(i * SLOTS, SLOTS)
        pltpu.make_async_copy(src.at[part], dst.at[part], r_sem).start()

    def send(src, dst, s_sem, r_sem, i, device):
        part = pl.ds(i * SLOTS, SLOTS)
        pltpu.make_async_remote_copy(
            src_ref=src.at[part], dst_ref=dst.at[part], send_sem=s_sem, recv_sem=r_sem,
            device_id=(section, device), device_id_type=MESH,
        ).start()

    def pack(kind, tick, side, q, dz):
        i = q * 8 + dz
        for r in range(SLOTS):
            s = i * SLOTS + r
            if kind == 0:
                send_a[tick, s] = blocks_a[tick][side][toks[side][tick, s]]
            else:
                rows = blocks_b[tick][side][toks[side][tick, s]].astype(jnp.float32)
                send_b[tick, s] = (rows * gates[side][tick, s]).astype(jnp.bfloat16)
        src, dst = ((send_a, recv_a), (send_b, recv_b))[kind]
        src, dst, s_sem = src.at[tick], dst.at[tick], send_sem.at[kind, tick]
        r_sem = (recv_a_sem, recv_b_sem)[kind].at[tick, q]
        left = (dz - SHIFT[side]) % 8
        if left != 0:
            send(src, dst, s_sem, r_sem, i, peer(me, q * 8 + left, 1))
            return

        @pl.when(q == 0)
        def _():
            stay(src, dst, r_sem, i)

        @pl.when(q > 0)
        def _():
            send(src, dst, s_sem, r_sem, i, peer(me, q * 8, 1))

    def pack_own(kind, tick):
        def body(q, carry):
            pack(kind, tick, OWN, q, 0)
            return carry

        lax.fori_loop(0, GROUPS, body, 0)

    def pack_sides(kind, tick, first=0, end=GROUPS // 2):
        def body(half, carry):
            for odd in range(2):
                q = half * 2 + odd
                for dz in range(1, 4):
                    pack(kind, tick, BEHIND, q, dz)
                    pack(kind, tick, AHEAD, q, 8 - dz)
                pack(kind, tick, (BEHIND, AHEAD)[odd], q, 4)
            return carry

        lax.fori_loop(first, end, body, 0)

    def wait_bytes(ref, sem):
        pltpu.make_async_copy(ref, ref, sem).wait()

    def to_rows(tiles, rows):
        by_slot[...] = tiles.astype(jnp.float32).reshape(GROUP_ROWS * TILES, LANES)
        for c in range(TILES):
            rows[:, lanes(c)] = by_slot[pl.ds(c, GROUP_ROWS, stride=TILES), :].astype(jnp.bfloat16)

    def experts(tick):
        def body(g, carry):
            part = pl.ds(g * GROUP_ROWS, GROUP_ROWS)
            wait_bytes(recv_a.at[tick, part], recv_a_sem.at[tick, g])
            wait_bytes(recv_b.at[tick, part], recv_b_sem.at[tick, g])
            to_rows(recv_a[tick, part], rows_a)
            to_rows(recv_b[tick, part], rows_b)
            normed = rows_a[...]
            pre_gate = jnp.dot(normed, wg[...], preferred_element_type=jnp.float32)
            pre_up = jnp.dot(normed, wu[...], preferred_element_type=jnp.float32)
            hidden_grad = contract_last(rows_b[...], wd[...])
            sigmoid = jax.nn.sigmoid(pre_gate)
            gate_grad = (
                hidden_grad * pre_up * sigmoid * (1.0 + pre_gate * (1.0 - sigmoid))
            ).astype(jnp.bfloat16)
            up_grad = (hidden_grad * pre_gate * sigmoid).astype(jnp.bfloat16)
            summed = contract_last(gate_grad, wg[...]) + contract_last(up_grad, wu[...])
            for c in range(TILES):
                by_slot[pl.ds(c, GROUP_ROWS, stride=TILES), :] = summed[:, lanes(c)]
            send_c[tick, part] = by_slot[...].reshape(GROUP_ROWS, TILES, LANES).astype(jnp.bfloat16)

            def give_back(j, inner):
                i = g * IN_GROUP + j

                @pl.when(i == 0)
                def _():
                    stay(send_c.at[tick], recv_c.at[tick], recv_c_sem.at[tick], i)

                @pl.when(i > 0)
                def _():
                    send(
                        send_c.at[tick], recv_c.at[tick], send_sem.at[2, tick], recv_c_sem.at[tick],
                        i, peer(me, i, -1),
                    )

                return inner

            lax.fori_loop(0, IN_GROUP, give_back, 0)
            return carry

        lax.fori_loop(0, GROUPS, body, 0)

    def combine(tick):
        wait_bytes(recv_c.at[tick], recv_c_sem.at[tick])

        def add(n, carry):
            for u in range(UNROLL):
                t = n * UNROLL + u
                by_token[pl.ds(pl.multiple_of(t * TILES, TILES), TILES), :] = recv_c[
                    tick, slot_ref[tick, 0, t]
                ].astype(jnp.float32) + recv_c[tick, slot_ref[tick, 1, t]].astype(jnp.float32)
            return carry

        lax.fori_loop(0, TOK // UNROLL, add, 0)
        for part in range(RELAY):
            first = part * RELAY_ROWS
            rows = slice(first, first + RELAY_ROWS)
            total = jnp.zeros((RELAY_ROWS, LANES), jnp.float32)
            for c in range(TILES):
                weighted = gain_ref[:, lanes(c)] * by_token[pl.ds(first * TILES + c, RELAY_ROWS, stride=TILES), :]
                total = total + x_ref[tick, rows, lanes(c)].astype(jnp.float32) * weighted
            project = jnp.sum(total, axis=1, keepdims=True) / D
            inverse = inverse_ref[tick, rows]
            cubed = inverse * inverse * inverse * project
            for c in range(TILES):
                weighted = gain_ref[:, lanes(c)] * by_token[pl.ds(first * TILES + c, RELAY_ROWS, stride=TILES), :]
                out_ref[tick, rows, lanes(c)] = (
                    current[rows, lanes(c)].astype(jnp.float32)
                    + inverse * weighted
                    - x_ref[tick, rows, lanes(c)].astype(jnp.float32) * cubed
                ).astype(jnp.bfloat16)
            if tick == 0:

                @pl.when(section > 0)
                def _():
                    relay(part).start()

    def relay(part):
        rows = pl.ds(part * RELAY_ROWS, RELAY_ROWS)
        return pltpu.make_async_remote_copy(
            src_ref=out_ref.at[0, rows],
            dst_ref=arrived.at[rows],
            send_sem=relay_send_sem.at[part],
            recv_sem=relay_recv_sem.at[part],
            device_id=(section - 1, me),
            device_id_type=MESH,
        )

    def make_tables():
        down = lax.broadcasted_iota(jnp.int32, (TOK, TOK), 0)
        across = lax.broadcasted_iota(jnp.int32, (TOK, TOK), 1)
        slot_at = lax.broadcasted_iota(jnp.int32, (TOK, ROWS), 1)
        token_less = lax.broadcasted_iota(jnp.int32, (TOK, ROWS), 0) - TOK

        def column(row):
            return jnp.sum(jnp.where(down == across, row, jnp.zeros_like(row)), axis=1, keepdims=True)

        x, y, z = me // 32, (me // 8) % 4, me % 8
        for tick in range(TICKS):
            chosen = [routes_ref[tick, k : k + 1, :] for k in range(2)]
            columns = [column(row) for row in chosen]
            token = jnp.zeros((1, ROWS), jnp.int32)
            gate = jnp.zeros((1, ROWS), jnp.float32)
            for k in range(2):
                rank = jnp.zeros((1, TOK), jnp.int32)
                for other in columns:
                    same = (other == chosen[k]) & (down < across)
                    rank = rank + jnp.sum(jnp.where(same, 1, 0), axis=0, keepdims=True)
                dx = ((chosen[k] >> 5) - x) & 1
                dy = ((chosen[k] >> 3) - y) & 3
                dz = (chosen[k] - z) & 7
                slot = ((dx << 5) + (dy << 3) + dz) * SLOTS + rank
                slot_made[tick, k : k + 1, :] = jnp.minimum(slot, ROWS - 1)
                held = column(slot) == slot_at
                gate_column = column(gates_ref[tick, k : k + 1, :].astype(jnp.float32))
                token = token + jnp.sum(jnp.where(held, token_less, 0), axis=0, keepdims=True)
                gate = gate + jnp.sum(jnp.where(held, gate_column, 0.0), axis=0, keepdims=True)
            tok_made[tick : tick + 1, :] = jnp.clip(token + TOK, 0, TOK)
            gate_made[tick : tick + 1, :] = gate

    current[...] = entering_ref[...]
    load_current(0)

    @pl.when(section == 0)
    def _():
        pl.semaphore_wait(barrier, 11)

    @pl.when(section > 0)
    def _():
        pl.semaphore_wait(barrier, 12)

    for i in ring_y:
        greet(greet_sem.at[0], i)
    start(block_copies(1, 0))
    load_normed(0)
    start(block_copies(0, 0))
    make_tables()
    made_copies = [
        pltpu.make_async_copy(made, held, made_sem.at[n])
        for n, (made, held) in enumerate(((tok_made, toks[OWN]), (gate_made, gates[OWN]), (slot_made, slot_ref)))
    ]
    start(made_copies)
    pl.semaphore_wait(greet_sem.at[0], 3)
    for i in ring_x:
        greet(greet_sem.at[1], i)
    for copy in made_copies:
        copy.wait()
    start(table_copies)
    load_normed(1)
    start(block_copies(0, 1))
    pl.semaphore_wait(greet_sem.at[1], 1)
    pack_own(1, 0)
    pack_own(0, 0)
    await_arrival(table_copies)
    await_arrival(block_copies(1, 0))
    pack_sides(1, 0)
    await_arrival(block_copies(0, 0))
    pack_sides(0, 0)
    for copy in weight_copies:
        copy.wait()
    experts(0)
    pack_own(0, 1)
    await_arrival(block_copies(0, 1))
    pack_sides(0, 1, 0, 2)
    combine(0)

    @pl.when(lower)
    def _():
        pack_sides(0, 1, 2, 4)

    @pl.when(section < last)
    def _():
        for part in range(RELAY):
            rows = pl.ds(part * RELAY_ROWS, RELAY_ROWS)
            wait_bytes(arrived.at[rows], relay_recv_sem.at[part])
        current[...] = arrived[...]

    @pl.when(section == last)
    def _():
        current[...] = fresh_ref[...]

    load_current(1)
    start(block_copies(1, 1))
    pack_own(1, 1)

    @pl.when(~lower)
    def _():
        pack_sides(0, 1, 2, 4)

    await_arrival(block_copies(1, 1))
    pack_sides(1, 1)
    experts(1)
    combine(1)

    @pl.when(section > 0)
    def _():
        for part in range(RELAY):
            relay(part).wait_send()

    for copy in table_copies:
        copy.wait_send()
    for kind in range(2):
        for tick in range(TICKS):
            for copy in block_copies(kind, tick):
                copy.wait_send()
    for kind, (sent, stayed) in enumerate(((send_a, 3), (send_b, 3), (send_c, 1))):
        for tick in range(TICKS):
            wait_bytes(sent.at[tick, pl.ds(stayed * SLOTS, ROWS - stayed * SLOTS)], send_sem.at[kind, tick])


def local(layer_input, entering, fresh, routes, gate_weights, norm_gain, w_gate, w_up, w_down):
    by_choice = [a[:, 0].transpose(0, 2, 1) for a in (routes, gate_weights)]
    vmem = pl.BlockSpec(memory_space=pltpu.VMEM)
    hbm = pl.BlockSpec(memory_space=pl.ANY)
    tiles = pltpu.VMEM((TICKS, ROWS, TILES, LANES), jnp.bfloat16)
    blocks = [[pltpu.VMEM((TOK + 1, TILES, LANES), jnp.bfloat16)] * 3] * TICKS
    out = pl.pallas_call(
        kernel,
        out_shape=jax.ShapeDtypeStruct((TICKS, TOK, D), jnp.bfloat16),
        in_specs=[vmem] * 6 + [hbm] * 3,
        out_specs=vmem,
        scratch_shapes=[
            pltpu.VMEM((D, FFE), jnp.bfloat16),
            pltpu.VMEM((D, FFE), jnp.bfloat16),
            pltpu.VMEM((FFE, D), jnp.bfloat16),
            tiles, tiles, tiles, tiles, tiles, tiles,
            blocks, blocks,
            [pltpu.SMEM((TICKS, ROWS), jnp.int32)] * 3,
            [pltpu.SMEM((TICKS, ROWS), jnp.float32)] * 3,
            pltpu.SMEM((TICKS, 2, TOK), jnp.int32),
            pltpu.VMEM((TICKS, ROWS), jnp.int32),
            pltpu.VMEM((TICKS, ROWS), jnp.float32),
            pltpu.VMEM((TICKS, 2, TOK), jnp.int32),
            pltpu.VMEM((TOK * TILES, LANES), jnp.float32),
            pltpu.VMEM((GROUP_ROWS * TILES, LANES), jnp.float32),
            pltpu.VMEM((GROUP_ROWS, D), jnp.bfloat16),
            pltpu.VMEM((GROUP_ROWS, D), jnp.bfloat16),
            pltpu.VMEM((TICKS, TOK, LANES), jnp.float32),
            pltpu.VMEM((TOK, D), jnp.bfloat16),
            pltpu.VMEM((TOK, D), jnp.bfloat16),
            pltpu.SemaphoreType.DMA((3,)),
            pltpu.SemaphoreType.DMA((3, TICKS)),
            pltpu.SemaphoreType.DMA((TICKS, GROUPS)),
            pltpu.SemaphoreType.DMA((TICKS, GROUPS)),
            pltpu.SemaphoreType.DMA((TICKS,)),
            pltpu.SemaphoreType.DMA((RELAY,)),
            pltpu.SemaphoreType.DMA((RELAY,)),
            pltpu.SemaphoreType.DMA((2, TICKS, 2)),
            pltpu.SemaphoreType.DMA((2, TICKS, 2)),
            pltpu.SemaphoreType.DMA((2, 2)),
            pltpu.SemaphoreType.DMA((2, 2)),
            pltpu.SemaphoreType.DMA((3,)),
            pltpu.SemaphoreType.REGULAR((2,)),
        ],
        compiler_params=pltpu.CompilerParams(
            collective_id=0, has_side_effects=True, vmem_limit_bytes=56 << 20
        ),
    )(*by_choice, layer_input[:, 0], entering[0], fresh[0], norm_gain, w_gate[0, 0], w_up[0, 0], w_down[0, 0])
    return out[:, None]


def solution(mesh):
    in_specs = (
        P(None, "section", "expert", None),
        P("section", "expert", None),
        P(None, "expert", None),
        P(None, "section", "expert", None),
        P(None, "section", "expert", None),
        P("section", None),
        P("section", "expert", None, None),
        P("section", "expert", None, None),
        P("section", "expert", None, None),
    )
    out_specs = P(None, "section", "expert", None)
    return jax.shard_map(local, mesh=mesh, in_specs=in_specs, out_specs=out_specs, check_vma=False)
```

```python
import functools

import jax
import jax.numpy as jnp
from jax import lax
from jax.experimental import pallas as pl
from jax.experimental.pallas import tpu as pltpu
from jax.sharding import PartitionSpec as P

D = 2048
FFE = 768
TICKS = 2
TOK = 128
PEERS = 64
SLOTS = 6
ROWS = PEERS * SLOTS
GROUPS = 8
IN_GROUP = PEERS // GROUPS
GROUP_ROWS = IN_GROUP * SLOTS
LANES = 128
TILES = D // LANES
RELAY = 4
RELAY_ROWS = TOK // RELAY
UNROLL = 8
PART_ROWS = 16
MESH = pl.DeviceIdType.MESH

OWN, BEHIND, AHEAD = range(3)
SHIFT = (0, 1, -1)


def peer(me, i, sign):
    dx, dy, dz = i // 32, (i // 8) % 4, i % 8
    x, y, z = me // 32, (me // 8) % 4, me % 8
    return ((x + dx) % 2) * 32 + ((y + sign * dy + 4) % 4) * 8 + (z + sign * dz + 8) % 8


def lanes(c):
    return slice(c * LANES, (c + 1) * LANES)


def contract_last(left, right):
    return lax.dot_general(
        left, right, (((1,), (1,)), ((), ())), preferred_element_type=jnp.float32
    )


def kernel(
    routes_ref, gates_ref, entering_ref, gain_ref, x_hbm, fresh_hbm, wg_hbm, wu_hbm, wd_hbm,
    out_ref,
    x_ref, fresh_ref, wg, wu, wd, send_a, send_b, send_c, recv_a, recv_b, recv_c, blocks_a, blocks_b, toks, gates, slot_ref,
    tok_made, gate_made, slot_made,
    by_token, by_slot, rows_a, rows_b, inverse_ref, current, arrived,
    row_sem, w_sem, send_sem, recv_a_sem, recv_b_sem, recv_c_sem, relay_send_sem, relay_recv_sem,
    block_send_sem, block_recv_sem, table_send_sem, table_recv_sem, made_sem, greet_sem,
):
    me = lax.axis_index("expert")
    section = lax.axis_index("section")
    last = lax.axis_size("section") - 1
    lower = section < 2

    barrier = pltpu.get_barrier_semaphore()

    def greet(sem, i):
        pl.semaphore_signal(sem, inc=1, device_id=(section, peer(me, i, 1)), device_id_type=MESH)

    ring_z, ring_y, ring_x = range(1, 8), (8, 16, 24), (32,)
    for i in (*ring_z, *ring_y, *ring_x):
        greet(barrier, i)

    @pl.when(section < last)
    def _():
        pl.semaphore_signal(barrier, inc=1, device_id=(section + 1, me), device_id_type=MESH)

    row_copies = [
        pltpu.make_async_copy(src, dst, row_sem.at[n])
        for n, (src, dst) in enumerate(
            ((x_hbm.at[0], x_ref.at[0]), (x_hbm.at[1], x_ref.at[1]), (fresh_hbm, fresh_ref))
        )
    ]
    for copy in row_copies:
        copy.start()
    weight_copies = [
        pltpu.make_async_copy(src, dst, w_sem.at[n])
        for n, (src, dst) in enumerate(((wg_hbm, wg), (wu_hbm, wu), (wd_hbm, wd)))
    ]
    for copy in weight_copies:
        copy.start()

    for tick_blocks in (*blocks_a, *blocks_b):
        for block in tick_blocks:
            block[TOK] = jnp.zeros((TILES, LANES), jnp.bfloat16)

    def store_block(block):
        for part in range(RELAY):
            rows = by_token[pl.ds(part * RELAY_ROWS * TILES, RELAY_ROWS * TILES), :]
            block[pl.ds(part * RELAY_ROWS, RELAY_ROWS)] = rows.reshape(RELAY_ROWS, TILES, LANES).astype(jnp.bfloat16)

    def load_normed(tick):
        total = jnp.zeros((TOK, LANES), jnp.float32)
        for c in range(TILES):
            x = x_ref[tick, :, lanes(c)].astype(jnp.float32)
            total = total + x * x
        inverse = lax.rsqrt(jnp.sum(total, axis=1, keepdims=True) / D + 1e-05)
        inverse_ref[tick] = jnp.broadcast_to(inverse, (TOK, LANES))
        for c in range(TILES):
            x = x_ref[tick, :, lanes(c)].astype(jnp.float32)
            by_token[pl.ds(c, TOK, stride=TILES), :] = x * inverse * gain_ref[:, lanes(c)]
        store_block(blocks_a[tick][OWN])

    def load_current(tick):
        for c in range(TILES):
            by_token[pl.ds(c, TOK, stride=TILES), :] = current[:, lanes(c)].astype(jnp.float32)
        store_block(blocks_b[tick][OWN])

    def along_z(src, dst, s_sem, r_sem, step):
        return pltpu.make_async_remote_copy(
            src_ref=src, dst_ref=dst, send_sem=s_sem, recv_sem=r_sem,
            device_id=(section, peer(me, 1, step)), device_id_type=MESH,
        )

    def start_blocks(kind, tick):
        blocks = (blocks_a, blocks_b)[kind][tick]

        def body(part, carry):
            rows = pl.ds(part * PART_ROWS, PART_ROWS)
            for side in (BEHIND, AHEAD):
                along_z(
                    blocks[OWN].at[rows], blocks[side].at[rows],
                    block_send_sem.at[kind, tick, side - 1], block_recv_sem.at[kind, tick, side - 1], SHIFT[side],
                ).start()
            return carry

        lax.fori_loop(0, TOK // PART_ROWS, body, 0)

    def await_blocks(kind, tick):
        blocks = (blocks_a, blocks_b)[kind][tick]
        for side in (BEHIND, AHEAD):
            wait_bytes(blocks[side].at[pl.ds(0, TOK)], block_recv_sem.at[kind, tick, side - 1])

    table_copies = [
        along_z(
            table[OWN], table[side],
            table_send_sem.at[n, side - 1], table_recv_sem.at[n, side - 1], SHIFT[side],
        )
        for n, table in enumerate((toks, gates))
        for side in (BEHIND, AHEAD)
    ]

    def start(copies):
        for copy in copies:
            copy.start()

    def await_arrival(copies):
        for copy in copies:
            copy.wait_recv()

    def stay(src, dst, r_sem, i):
        part = pl.ds(i * SLOTS, SLOTS)
        pltpu.make_async_copy(src.at[part], dst.at[part], r_sem).start()

    def send(src, dst, s_sem, r_sem, i, device):
        part = pl.ds(i * SLOTS, SLOTS)
        pltpu.make_async_remote_copy(
            src_ref=src.at[part], dst_ref=dst.at[part], send_sem=s_sem, recv_sem=r_sem,
            device_id=(section, device), device_id_type=MESH,
        ).start()

    def pack(kind, tick, side, q, dz):
        i = q * 8 + dz
        for r in range(SLOTS):
            s = i * SLOTS + r
            if kind == 0:
                send_a[tick, s] = blocks_a[tick][side][toks[side][tick, s]]
            else:
                rows = blocks_b[tick][side][toks[side][tick, s]].astype(jnp.float32)
                send_b[tick, s] = (rows * gates[side][tick, s]).astype(jnp.bfloat16)
        src, dst = ((send_a, recv_a), (send_b, recv_b))[kind]
        src, dst, s_sem = src.at[tick], dst.at[tick], send_sem.at[kind, tick]
        r_sem = (recv_a_sem, recv_b_sem)[kind].at[tick, q]
        left = (dz - SHIFT[side]) % 8
        if left != 0:
            send(src, dst, s_sem, r_sem, i, peer(me, q * 8 + left, 1))
            return

        @pl.when(q == 0)
        def _():
            stay(src, dst, r_sem, i)

        @pl.when(q > 0)
        def _():
            send(src, dst, s_sem, r_sem, i, peer(me, q * 8, 1))

    def pack_own(kind, tick):
        def body(q, carry):
            pack(kind, tick, OWN, q, 0)
            return carry

        lax.fori_loop(0, GROUPS, body, 0)

    def pack_sides(kind, tick, first=0, end=GROUPS // 2):
        def body(half, carry):
            for odd in range(2):
                q = half * 2 + odd
                for dz in range(1, 4):
                    pack(kind, tick, BEHIND, q, dz)
                    pack(kind, tick, AHEAD, q, 8 - dz)
                pack(kind, tick, (BEHIND, AHEAD)[odd], q, 4)
            return carry

        lax.fori_loop(first, end, body, 0)

    def wait_bytes(ref, sem):
        pltpu.make_async_copy(ref, ref, sem).wait()

    def to_rows(tiles, rows):
        by_slot[...] = tiles.astype(jnp.float32).reshape(GROUP_ROWS * TILES, LANES)
        for c in range(TILES):
            rows[:, lanes(c)] = by_slot[pl.ds(c, GROUP_ROWS, stride=TILES), :].astype(jnp.bfloat16)

    def experts(tick):
        def body(g, carry):
            part = pl.ds(g * GROUP_ROWS, GROUP_ROWS)
            wait_bytes(recv_a.at[tick, part], recv_a_sem.at[tick, g])
            wait_bytes(recv_b.at[tick, part], recv_b_sem.at[tick, g])
            to_rows(recv_a[tick, part], rows_a)
            to_rows(recv_b[tick, part], rows_b)
            normed = rows_a[...]
            pre_gate = jnp.dot(normed, wg[...], preferred_element_type=jnp.float32)
            pre_up = jnp.dot(normed, wu[...], preferred_element_type=jnp.float32)
            hidden_grad = contract_last(rows_b[...], wd[...])
            sigmoid = jax.nn.sigmoid(pre_gate)
            gate_grad = (
                hidden_grad * pre_up * sigmoid * (1.0 + pre_gate * (1.0 - sigmoid))
            ).astype(jnp.bfloat16)
            up_grad = (hidden_grad * pre_gate * sigmoid).astype(jnp.bfloat16)
            summed = contract_last(gate_grad, wg[...]) + contract_last(up_grad, wu[...])
            for c in range(TILES):
                by_slot[pl.ds(c, GROUP_ROWS, stride=TILES), :] = summed[:, lanes(c)]
            send_c[tick, part] = by_slot[...].reshape(GROUP_ROWS, TILES, LANES).astype(jnp.bfloat16)

            def give_back(j, inner):
                i = g * IN_GROUP + j

                @pl.when(i == 0)
                def _():
                    stay(send_c.at[tick], recv_c.at[tick], recv_c_sem.at[tick], i)

                @pl.when(i > 0)
                def _():
                    send(
                        send_c.at[tick], recv_c.at[tick], send_sem.at[2, tick], recv_c_sem.at[tick],
                        i, peer(me, i, -1),
                    )

                return inner

            lax.fori_loop(0, IN_GROUP, give_back, 0)
            return carry

        lax.fori_loop(0, GROUPS, body, 0)

    def combine(tick):
        wait_bytes(recv_c.at[tick], recv_c_sem.at[tick])

        def add(n, carry):
            for u in range(UNROLL):
                t = n * UNROLL + u
                by_token[pl.ds(pl.multiple_of(t * TILES, TILES), TILES), :] = recv_c[
                    tick, slot_ref[tick, 0, t]
                ].astype(jnp.float32) + recv_c[tick, slot_ref[tick, 1, t]].astype(jnp.float32)
            return carry

        lax.fori_loop(0, TOK // UNROLL, add, 0)
        for part in range(RELAY):
            first = part * RELAY_ROWS
            rows = slice(first, first + RELAY_ROWS)
            total = jnp.zeros((RELAY_ROWS, LANES), jnp.float32)
            for c in range(TILES):
                weighted = gain_ref[:, lanes(c)] * by_token[pl.ds(first * TILES + c, RELAY_ROWS, stride=TILES), :]
                total = total + x_ref[tick, rows, lanes(c)].astype(jnp.float32) * weighted
            project = jnp.sum(total, axis=1, keepdims=True) / D
            inverse = inverse_ref[tick, rows]
            cubed = inverse * inverse * inverse * project
            for c in range(TILES):
                weighted = gain_ref[:, lanes(c)] * by_token[pl.ds(first * TILES + c, RELAY_ROWS, stride=TILES), :]
                out_ref[tick, rows, lanes(c)] = (
                    current[rows, lanes(c)].astype(jnp.float32)
                    + inverse * weighted
                    - x_ref[tick, rows, lanes(c)].astype(jnp.float32) * cubed
                ).astype(jnp.bfloat16)
            if tick == 0:

                @pl.when(section > 0)
                def _():
                    relay(part).start()

    def relay(part):
        rows = pl.ds(part * RELAY_ROWS, RELAY_ROWS)
        return pltpu.make_async_remote_copy(
            src_ref=out_ref.at[0, rows],
            dst_ref=arrived.at[rows],
            send_sem=relay_send_sem.at[part],
            recv_sem=relay_recv_sem.at[part],
            device_id=(section - 1, me),
            device_id_type=MESH,
        )

    def make_tables():
        down = lax.broadcasted_iota(jnp.int32, (TOK, TOK), 0)
        across = lax.broadcasted_iota(jnp.int32, (TOK, TOK), 1)
        slot_at = lax.broadcasted_iota(jnp.int32, (TOK, ROWS), 1)
        token_less = lax.broadcasted_iota(jnp.int32, (TOK, ROWS), 0) - TOK

        def column(row):
            return jnp.sum(jnp.where(down == across, row, jnp.zeros_like(row)), axis=1, keepdims=True)

        x, y, z = me // 32, (me // 8) % 4, me % 8
        for tick in range(TICKS):
            chosen = [routes_ref[tick, k : k + 1, :] for k in range(2)]
            columns = [column(row) for row in chosen]
            token = jnp.zeros((1, ROWS), jnp.int32)
            gate = jnp.zeros((1, ROWS), jnp.float32)
            for k in range(2):
                rank = jnp.zeros((1, TOK), jnp.int32)
                for other in columns:
                    same = (other == chosen[k]) & (down < across)
                    rank = rank + jnp.sum(jnp.where(same, 1, 0), axis=0, keepdims=True)
                dx = ((chosen[k] >> 5) - x) & 1
                dy = ((chosen[k] >> 3) - y) & 3
                dz = (chosen[k] - z) & 7
                slot = ((dx << 5) + (dy << 3) + dz) * SLOTS + rank
                slot_made[tick, k : k + 1, :] = jnp.minimum(slot, ROWS - 1)
                held = column(slot) == slot_at
                gate_column = column(gates_ref[tick, k : k + 1, :].astype(jnp.float32))
                token = token + jnp.sum(jnp.where(held, token_less, 0), axis=0, keepdims=True)
                gate = gate + jnp.sum(jnp.where(held, gate_column, 0.0), axis=0, keepdims=True)
            tok_made[tick : tick + 1, :] = jnp.clip(token + TOK, 0, TOK)
            gate_made[tick : tick + 1, :] = gate

    current[...] = entering_ref[...]
    load_current(0)

    @pl.when(section == 0)
    def _():
        pl.semaphore_wait(barrier, 11)

    @pl.when(section > 0)
    def _():
        pl.semaphore_wait(barrier, 12)

    for i in ring_y:
        greet(greet_sem.at[0], i)
    start_blocks(1, 0)
    row_copies[0].wait()
    load_normed(0)
    start_blocks(0, 0)
    make_tables()
    made_copies = [
        pltpu.make_async_copy(made, held, made_sem.at[n])
        for n, (made, held) in enumerate(((tok_made, toks[OWN]), (gate_made, gates[OWN]), (slot_made, slot_ref)))
    ]
    start(made_copies)
    pl.semaphore_wait(greet_sem.at[0], 3)
    for i in ring_x:
        greet(greet_sem.at[1], i)
    for copy in made_copies:
        copy.wait()
    start(table_copies)
    row_copies[1].wait()
    load_normed(1)
    start_blocks(0, 1)
    pl.semaphore_wait(greet_sem.at[1], 1)
    pack_own(1, 0)
    pack_own(0, 0)
    await_arrival(table_copies)
    await_blocks(1, 0)
    pack_sides(1, 0)
    await_blocks(0, 0)
    pack_sides(0, 0)
    for copy in (row_copies[2], *weight_copies):
        copy.wait()
    experts(0)
    pack_own(0, 1)
    await_blocks(0, 1)
    pack_sides(0, 1, 0, 2)
    combine(0)

    @pl.when(lower)
    def _():
        pack_sides(0, 1, 2, 4)

    @pl.when(section < last)
    def _():
        for part in range(RELAY):
            rows = pl.ds(part * RELAY_ROWS, RELAY_ROWS)
            wait_bytes(arrived.at[rows], relay_recv_sem.at[part])
        current[...] = arrived[...]

    @pl.when(section == last)
    def _():
        current[...] = fresh_ref[...]

    load_current(1)
    start_blocks(1, 1)
    pack_own(1, 1)

    @pl.when(~lower)
    def _():
        pack_sides(0, 1, 2, 4)

    await_blocks(1, 1)
    pack_sides(1, 1)
    experts(1)
    combine(1)

    @pl.when(section > 0)
    def _():
        for part in range(RELAY):
            relay(part).wait_send()

    for copy in table_copies:
        copy.wait_send()
    for kind in range(2):
        for tick in range(TICKS):
            for side in (BEHIND, AHEAD):
                own = (blocks_a, blocks_b)[kind][tick][OWN]
                wait_bytes(own.at[pl.ds(0, TOK)], block_send_sem.at[kind, tick, side - 1])
    for kind, (sent, stayed) in enumerate(((send_a, 3), (send_b, 3), (send_c, 1))):
        for tick in range(TICKS):
            wait_bytes(sent.at[tick, pl.ds(stayed * SLOTS, ROWS - stayed * SLOTS)], send_sem.at[kind, tick])


def local(layer_input, entering, fresh, routes, gate_weights, norm_gain, w_gate, w_up, w_down):
    by_choice = [a[:, 0].transpose(0, 2, 1) for a in (routes, gate_weights)]
    vmem = pl.BlockSpec(memory_space=pltpu.VMEM)
    hbm = pl.BlockSpec(memory_space=pl.ANY)
    tiles = pltpu.VMEM((TICKS, ROWS, TILES, LANES), jnp.bfloat16)
    blocks = [[pltpu.VMEM((TOK + 1, TILES, LANES), jnp.bfloat16)] * 3] * TICKS
    out = pl.pallas_call(
        kernel,
        out_shape=jax.ShapeDtypeStruct((TICKS, TOK, D), jnp.bfloat16),
        in_specs=[vmem] * 4 + [hbm] * 5,
        out_specs=vmem,
        scratch_shapes=[
            pltpu.VMEM((TICKS, TOK, D), jnp.bfloat16),
            pltpu.VMEM((TOK, D), jnp.bfloat16),
            pltpu.VMEM((D, FFE), jnp.bfloat16),
            pltpu.VMEM((D, FFE), jnp.bfloat16),
            pltpu.VMEM((FFE, D), jnp.bfloat16),
            tiles, tiles, tiles, tiles, tiles, tiles,
            blocks, blocks,
            [pltpu.SMEM((TICKS, ROWS), jnp.int32)] * 3,
            [pltpu.SMEM((TICKS, ROWS), jnp.float32)] * 3,
            pltpu.SMEM((TICKS, 2, TOK), jnp.int32),
            pltpu.VMEM((TICKS, ROWS), jnp.int32),
            pltpu.VMEM((TICKS, ROWS), jnp.float32),
            pltpu.VMEM((TICKS, 2, TOK), jnp.int32),
            pltpu.VMEM((TOK * TILES, LANES), jnp.float32),
            pltpu.VMEM((GROUP_ROWS * TILES, LANES), jnp.float32),
            pltpu.VMEM((GROUP_ROWS, D), jnp.bfloat16),
            pltpu.VMEM((GROUP_ROWS, D), jnp.bfloat16),
            pltpu.VMEM((TICKS, TOK, LANES), jnp.float32),
            pltpu.VMEM((TOK, D), jnp.bfloat16),
            pltpu.VMEM((TOK, D), jnp.bfloat16),
            pltpu.SemaphoreType.DMA((3,)),
            pltpu.SemaphoreType.DMA((3,)),
            pltpu.SemaphoreType.DMA((3, TICKS)),
            pltpu.SemaphoreType.DMA((TICKS, GROUPS)),
            pltpu.SemaphoreType.DMA((TICKS, GROUPS)),
            pltpu.SemaphoreType.DMA((TICKS,)),
            pltpu.SemaphoreType.DMA((RELAY,)),
            pltpu.SemaphoreType.DMA((RELAY,)),
            pltpu.SemaphoreType.DMA((2, TICKS, 2)),
            pltpu.SemaphoreType.DMA((2, TICKS, 2)),
            pltpu.SemaphoreType.DMA((2, 2)),
            pltpu.SemaphoreType.DMA((2, 2)),
            pltpu.SemaphoreType.DMA((3,)),
            pltpu.SemaphoreType.REGULAR((2,)),
        ],
        compiler_params=pltpu.CompilerParams(
            collective_id=0, has_side_effects=True, vmem_limit_bytes=56 << 20
        ),
    )(*by_choice, entering[0], norm_gain, layer_input[:, 0], fresh[0], w_gate[0, 0], w_up[0, 0], w_down[0, 0])
    return out[:, None]


def solution(mesh):
    in_specs = (
        P(None, "section", "expert", None),
        P("section", "expert", None),
        P(None, "expert", None),
        P(None, "section", "expert", None),
        P(None, "section", "expert", None),
        P("section", None),
        P("section", "expert", None, None),
        P("section", "expert", None, None),
        P("section", "expert", None, None),
    )
    out_specs = P(None, "section", "expert", None)
    return jax.shard_map(local, mesh=mesh, in_specs=in_specs, out_specs=out_specs, check_vma=False)
```
